32 devices in a mesh: group: 8 (over y, x, core), tensor: 4 (over z).
Axes of the slice: x: 2, y: 2, z: 4, core: 2. Of those that a mesh axis runs over, the one named last changes fastest.
Arguments:
- retrieved: bfloat16 [4096, 2, 2560], P('group', None, 'tensor'), may hold values from -6 to 6
- branch_states: bfloat16 [4096, 2, 2560], P('group', None, 'tensor'), may hold values from -62 to 62
- out_grad: bfloat16 [4096, 2, 2560], P('group', None, 'tensor'), may hold values from -6 to 6
- key_weight: bfloat16 [2, 2560, 2560], P(None, None, 'tensor'), may hold values from -0.125 to 0.125
- value_weight: bfloat16 [2560, 2560], P(None, 'tensor'), may hold values from -0.125 to 0.125
- key_grad_acc: float32 [2, 2560, 2560], P(None, 'group', 'tensor'), may hold values from -6 to 6
- value_grad_acc: float32 [2560, 2560], P('group', 'tensor'), may hold values from -6 to 6
- row_index: int32 [4096, 2], P('group'), may hold values from 0 to 2047, as said below
- row_tier: int32 [2048], P('group'), may hold values 0 or 1
- adam_mean: float32 [2048, 2560], P('group', 'tensor'), may hold values from -3 to 3
- adam_second: float32 [2048, 2560], P('group', 'tensor'), may hold values from 0.01 to 1
Outputs:
- key_grad: float32 [2, 2560, 2560], P(None, 'group', 'tensor')
- value_grad: float32 [2560, 2560], P('group', 'tensor')
- new_mean: float32 [2048, 2560], P('group', 'tensor')
- new_second: float32 [2048, 2560], P('group', 'tensor')
- row_step: float32 [2048, 2560], P('group', 'tensor')
The draws below stay inside these ranges and needn't reach their ends.
Inputs may be any that keep to these rules, and one draw needn't show every extreme that they name: `row_index`: rows o * 256 to (o + 1) * 256 - 1 belong to owner o. Of the 1024 entries of each group's 512 tokens, at most 128 belong to one owner, and one owner receives exactly 128 entries from every group.
All inputs are finite; a program needn't handle non-finite values. No bound on the sum of `row_tier` on one device may be relied on, other than what follows from the above.
Results may differ from the reference program's by a relative error of at most 0.0054.
Values may be sent and summed in bfloat16 or wider, within the bound.
No kernel may reach another device: no remote copies, remote signals or barrier semaphores. Data moves between devices by JAX's collectives and lax.ppermute only.
A program may use at most 128 MiB of HBM per device.

```python
import math
import jax
import jax.numpy as jnp
from jax import lax

D = 2560
KEYS = 2
NGRAM = 2
TOK = 512
CAP = 128
ROWS = 2048
TOKENS = 4096


def draw_branch_states(key, part):
    sub_keys = jax.random.split(key, 3)
    row_scale = jnp.exp(jax.random.uniform(sub_keys[1], (TOKENS, KEYS, 1), jnp.float32, -1.15, 1.15))
    col_scale = jnp.exp(jax.random.uniform(sub_keys[2], (1, 1, D), jnp.float32, -1.15, 1.15))
    base_noise = jnp.clip(jax.random.normal(sub_keys[0], (TOKENS, KEYS, D), jnp.float32), -6.0, 6.0)
    return (base_noise * row_scale * col_scale).astype(jnp.bfloat16)


def draw_row_index(key, part):
    groups = TOKENS // TOK
    owned_rows = ROWS // groups
    entry_count = TOK * NGRAM
    hot_owner = jax.random.randint(jax.random.fold_in(key, 7), (), 0, groups).astype(jnp.int32)

    def one_group(group_id):
        group_key = jax.random.fold_in(jax.random.fold_in(key, 11), group_id)
        pool_key, order_key, local_key = jax.random.split(group_key, 3)
        slot_pool = jax.random.permutation(pool_key, (groups - 1) * CAP)[:entry_count - CAP].astype(jnp.int32)
        other_owner = slot_pool // CAP
        other_owner = other_owner + (other_owner >= hot_owner).astype(jnp.int32)
        owners = jnp.concatenate([jnp.full((CAP,), 1, jnp.int32) * hot_owner, other_owner])
        owners = jax.random.permutation(order_key, owners)
        local_row = jax.random.randint(local_key, (entry_count,), 0, owned_rows).astype(jnp.int32)
        return (owners * owned_rows + local_row).reshape(TOK, NGRAM)
    result = jax.vmap(one_group)(jnp.arange(groups, dtype=jnp.int32))
    return result.reshape(TOKENS, NGRAM).astype(jnp.int32)


def plant(values, rng, least, largest):
    dims = values.shape
    spot = [jax.random.randint(jax.random.fold_in(rng, axis), (), 0, dims[axis]) for axis in range(len(dims))]
    values = values.at[tuple(spot)].set(least)
    longest = dims.index(max(dims))
    spot[longest] = (spot[longest] + 1) % dims[longest]
    return values.at[tuple(spot)].set(largest)


def levels(stream_key, dims, cuts, least, top_value):
    def one(position, blocks):
        steps = jax.random.uniform(jax.random.fold_in(jax.random.fold_in(stream_key, 6), position), (blocks,), jnp.float32, least / len(cuts), top_value / len(cuts))
        return jnp.repeat(jnp.exp(steps), dims[position] // blocks).reshape((-1,) + (1,) * (len(dims) - position - 1))

    factor_of = one(*cuts[0])
    for cut in cuts[1:]:
        factor_of = factor_of * one(*cut)
    return factor_of


def gaussian(stream_key, extent, deviation, bound, shards=(), kind=jnp.bfloat16):
    values = jax.random.normal(stream_key, extent, jnp.float32) * deviation
    if len(shards) > 0:
        values = levels(stream_key, extent, shards, -0.22, 0.18) * values
    return jnp.clip(values, min=-bound, max=bound).astype(kind)


def setup_inputs(seed: int = 0) -> dict:
    splits = jax.random.split(jax.random.key(seed), 12)
    return {
        "retrieved": gaussian(splits[0], (TOKENS, NGRAM, D), 1.0, 6.0, ((0, 8), (2, 4))),
        "branch_states": draw_branch_states(jax.random.fold_in(splits[11], 71), 0),
        "out_grad": gaussian(splits[2], (TOKENS, KEYS, D), 1.0, 6.0, ((0, 8), (2, 4))),
        "key_weight": gaussian(splits[3], (KEYS, D, D), D ** -0.5, 0.125, ((2, 4),)),
        "value_weight": gaussian(splits[4], (D, D), D ** -0.5, 0.125, ((1, 4),)),
        "key_grad_acc": gaussian(splits[5], (KEYS, D, D), 1.0, 6.0, ((1, 8), (2, 4)), jnp.float32),
        "value_grad_acc": gaussian(splits[6], (D, D), 1.0, 6.0, ((0, 8), (1, 4)), jnp.float32),
        "row_index": draw_row_index(jax.random.fold_in(splits[11], 71), 0),
        "row_tier": plant((jax.random.randint(splits[8], (ROWS,), 0, 4) < 1).astype(jnp.int32), jax.random.fold_in(splits[8], 1), 0, 1),
        "adam_mean": gaussian(splits[9], (ROWS, D), 0.2, 3.0, ((0, 8), (1, 4)), jnp.float32),
        "adam_second": jnp.clip(jnp.exp(math.log(1.0) - 4.6051702 * jax.random.uniform(splits[10], (ROWS, D), jnp.float32) ** levels(splits[10], (ROWS, D), ((0, 8), (1, 4)), -0.2, 0.2)), 0.01, 1.0),
    }


EPS_NORM = 1e-06
EPS_ADAM = 1e-08
FIRST_BIAS = 1.0 - 0.9 ** 10
SECOND_BIAS = 1.0 - 0.95 ** 10

def reference(retrieved, branch_states, out_grad, key_weight, value_weight, key_grad_acc, value_grad_acc, row_index, row_tier, adam_mean, adam_second):
    memory = lax.optimization_barrier(jnp.sum(retrieved.astype(jnp.float32), axis=1)).astype(jnp.bfloat16)
    memory_wide = memory.astype(jnp.float32)
    key_vals = jnp.einsum('td,jdc->tjc', memory_wide, key_weight.astype(jnp.float32))
    values = jnp.dot(memory, value_weight, preferred_element_type=jnp.float32)
    states = branch_states.astype(jnp.float32)
    grads_out = out_grad.astype(jnp.float32)
    state_sq = lax.optimization_barrier(jnp.mean(states * states, axis=-1))
    key_sq = lax.optimization_barrier(jnp.mean(key_vals * key_vals, axis=-1))
    cross_dot = lax.optimization_barrier(jnp.sum(states * key_vals, axis=-1))
    out_dot = lax.optimization_barrier(jnp.sum(grads_out * values[:, None, :], axis=-1))
    root_width = jnp.sqrt(jnp.float32(D))
    state_rs = lax.rsqrt(state_sq + EPS_NORM)
    key_rs = lax.rsqrt(key_sq + EPS_NORM)
    scores = cross_dot * state_rs * key_rs / root_width
    gate_val = jax.nn.sigmoid(scores)
    dscore = out_dot * gate_val * (1.0 - gate_val)
    key_cot = ((key_rs * dscore / root_width)[..., None] * (states * state_rs[..., None] - key_vals * (key_rs * scores / root_width)[..., None])).astype(jnp.bfloat16)
    value_cot = lax.optimization_barrier(jnp.sum(gate_val[..., None] * grads_out, axis=1)).astype(jnp.bfloat16)
    key_cot_wide = key_cot.astype(jnp.float32)
    value_cot_wide = value_cot.astype(jnp.float32)
    key_grad = key_grad_acc + jnp.einsum('td,tjc->jdc', memory_wide, key_cot_wide)
    value_grad = value_grad_acc + jnp.dot(memory.T, value_cot, preferred_element_type=jnp.float32)
    memory_cot = jnp.einsum('tjc,jdc->td', key_cot_wide, key_weight.astype(jnp.float32))
    memory_cot = memory_cot + jnp.dot(value_cot, value_weight.T, preferred_element_type=jnp.float32)
    entry_grad = jnp.repeat(memory_cot, NGRAM, axis=0)
    row_grad = jax.ops.segment_sum(entry_grad, row_index.reshape(-1).astype(jnp.int32), num_segments=ROWS)
    row_sq = lax.optimization_barrier(jnp.mean(row_grad * row_grad, axis=1))
    is_hot = (row_tier == 1)[:, None]
    mean_hot = 0.9 * adam_mean + 0.1 * row_grad
    second_hot = 0.95 * adam_second + 0.05 * row_grad * row_grad
    step_hot = mean_hot / FIRST_BIAS / (jnp.sqrt(second_hot / SECOND_BIAS) + EPS_ADAM)
    step_cold = row_grad * lax.rsqrt(row_sq + EPS_NORM)[:, None]
    new_mean = jnp.where(is_hot, mean_hot, adam_mean)
    new_second = jnp.where(is_hot, second_hot, adam_second)
    row_step = jnp.where(is_hot, step_hot, step_cold)
    return (key_grad, value_grad, new_mean, new_second, row_step)
```

```python
import functools

import jax
import jax.numpy as jnp
from jax import lax
from jax.experimental import pallas as pl
from jax.experimental.pallas import tpu as pltpu
from jax.sharding import PartitionSpec as P

CAP = 128
HALVES = 2
VMEM_BYTES = 48 * 1024 * 1024


EPS_NORM = 1e-06
EPS_ADAM = 1e-08
FIRST_BIAS = 1.0 - 0.9**10
SECOND_BIAS = 1.0 - 0.95**10

F32, BF16 = jnp.float32, jnp.bfloat16


def params():
    return pltpu.CompilerParams(vmem_limit_bytes=VMEM_BYTES)


def cost(macs, nbytes):
    return pl.CostEstimate(flops=2 * macs, bytes_accessed=nbytes, transcendentals=0)


def ring_device(place, size):
    return jnp.where(2 * place < size, 2 * place, 2 * (size - place) - 1)


def ring_place(device, size):
    return jnp.where(device % 2 == 0, device // 2, size - 1 - device // 2)


def ring_pass(part, axis):
    size = lax.axis_size(axis)
    order = list(range(0, size, 2)) + list(range(1, size, 2))[::-1]
    return lax.ppermute(part, axis, [(order[i], order[(i + 1) % size]) for i in range(size)])


def others_over(axis, part):
    size = lax.axis_size(axis)
    return [
        lax.ppermute(part, axis, [(i, (i + step) % size) for i in range(size)])
        for step in range(1, size)
    ]


def swap_over(axis, bit, part):
    size = lax.axis_size(axis)
    return lax.ppermute(part, axis, [(i, i ^ bit) for i in range(size)])


def forward_kernel(first, last, shard_ref, *refs):
    refs = list(refs)
    parts = [refs.pop(0) for _ in range(HALVES)]
    key_ref, value_ref = refs.pop(0), refs.pop(0)
    if not first:
        acc_ref = refs.pop(0)
        refs.pop(0)
    if last:
        state_ref, grad_ref = refs.pop(0), refs.pop(0)
    out_ref, turned_ref = refs.pop(0), refs.pop(0)
    key_count = key_ref.shape[0]

    def body(part):
        memory = part[...]
        turned_ref[...] = memory.T
        vals = []
        for j in range(key_count + 1):
            weight = key_ref[j] if j < key_count else value_ref[...]
            val = jnp.dot(memory, weight, preferred_element_type=F32)
            if not first:
                val = val + acc_ref[j]
            vals.append(val)
            if j < key_count or not last:
                out_ref[j] = val
        if last:
            states = [state_ref[j].astype(F32) for j in range(key_count)]
            sums = [jnp.sum(s * s, axis=1, keepdims=True) for s in states]
            sums += [jnp.sum(k * k, axis=1, keepdims=True) for k in vals[:-1]]
            sums += [jnp.sum(s * k, axis=1, keepdims=True) for s, k in zip(states, vals)]
            sums += [
                jnp.sum(grad_ref[j].astype(F32) * vals[-1], axis=1, keepdims=True)
                for j in range(key_count)
            ]
            lane = lax.broadcasted_iota(jnp.int32, (memory.shape[0], 128), 1)
            table = jnp.zeros((memory.shape[0], 128), F32)
            for i, s in enumerate(sums):
                table = jnp.where(lane == i, s, table)
            refs[0][...] = table.T[: 4 * key_count]

    for h in range(HALVES):
        pl.when(pl.program_id(0) == h)(functools.partial(body, parts[h]))


def forward(shard, parts, key_weight, value_weight, carry, extra):
    half, width = parts[0].shape
    key_count, model_width, _ = key_weight.shape
    tok_count = half * HALVES
    first, last = carry is None, extra is not None
    whole = pl.BlockSpec((half, width), lambda i, s: (0, 0))
    in_specs = [whole] * HALVES + [
        pl.BlockSpec((key_count, width, width), lambda i, s: (0, s[0], 0)),
        pl.BlockSpec((width, width), lambda i, s: (s[0], 0)),
    ]
    args = [shard, *parts, key_weight, value_weight]
    aliases = {}
    acc_spec = pl.BlockSpec((key_count + 1, half, width), lambda i, s: (0, i, 0))
    if not first:
        in_specs += [acc_spec, pl.BlockSpec(memory_space=pl.ANY)]
        args += list(carry)
        aliases = {len(args) - 1: 1}
        if not last:
            aliases[len(args) - 2] = 0
    pair = pl.BlockSpec((key_count, half, width), lambda i, s: (0, i, 0))
    if last:
        in_specs += [pair, pair]
        args += list(extra)
    out_count = key_count if last else key_count + 1
    out_specs = [
        pair if last else acc_spec,
        pl.BlockSpec((width, half), lambda i, s: (s[0], i)),
    ]
    out_shape = [
        jax.ShapeDtypeStruct((out_count, tok_count, width), F32),
        jax.ShapeDtypeStruct((model_width, tok_count), BF16),
    ]
    if last:
        out_specs.append(pl.BlockSpec((4 * key_count, half), lambda i, s: (0, i)))
        out_shape.append(jax.ShapeDtypeStruct((4 * key_count, tok_count), F32))
    return pl.pallas_call(
        functools.partial(forward_kernel, first, last),
        grid_spec=pltpu.PrefetchScalarGridSpec(
            num_scalar_prefetch=1, grid=(HALVES,), in_specs=in_specs, out_specs=out_specs
        ),
        out_shape=out_shape,
        input_output_aliases=aliases,
        compiler_params=params(),
        cost_estimate=cost(
            tok_count * width * width * (key_count + 1), 14 * tok_count * width * (key_count + 1)
        ),
        name="forward_last" if last else "forward_step",
    )(*args)


def back_term(cots, key_ref, value_ref):
    nt = (((1,), (1,)), ((), ()))
    term = lax.dot_general(cots[-1], value_ref[...], nt, preferred_element_type=F32)
    for j in range(key_ref.shape[0]):
        term = term + lax.dot_general(cots[j], key_ref[j], nt, preferred_element_type=F32)
    return term


def cot_kernel(sums_count, model_width, shard_ref, *refs):
    sum_refs = refs[:sums_count]
    val_ref, state_ref, grad_ref, key_ref, value_ref, joined_ref, term_ref = refs[sums_count:]
    key_count, half, width = val_ref.shape
    total = sum_refs[0][...]
    for ref in sum_refs[1:]:
        total = total + ref[...]
    root_width = jnp.sqrt(F32(model_width))
    state_sum, key_sum, cross_dot, out_dot = (
        total[i * key_count : (i + 1) * key_count] for i in range(4)
    )
    state_rs = lax.rsqrt(state_sum / model_width + EPS_NORM)
    key_rs = lax.rsqrt(key_sum / model_width + EPS_NORM)
    scores = cross_dot * state_rs * key_rs / root_width
    gate_val = 1.0 / (1.0 + jnp.exp(-scores))
    dscore = out_dot * gate_val * (1.0 - gate_val)
    lead = key_rs * dscore / root_width
    slope = key_rs * scores / root_width
    rows = jnp.concatenate(
        [lead, state_rs, slope, gate_val, jnp.zeros((128 - 4 * key_count, half), F32)], axis=0
    )
    table = rows.T
    column = lambda kind, j: table[:, kind * key_count + j : kind * key_count + j + 1]
    cots = []
    value_cot = None
    for j in range(key_count):
        inner = state_ref[j].astype(F32) * column(1, j) - val_ref[j] * column(2, j)
        cots.append((column(0, j) * inner).astype(BF16))
        gated = column(3, j) * grad_ref[j].astype(F32)
        value_cot = gated if value_cot is None else value_cot + gated
    cots.append(value_cot.astype(BF16))
    for j in range(key_count + 1):
        joined_ref[:, j * width : (j + 1) * width] = cots[j]
    term_ref[...] = back_term(cots, key_ref, value_ref).astype(BF16)


def cotangents(shard, sums, vals, states, grads, key_weight, value_weight):
    key_count, tok_count, width = vals.shape
    model_width = value_weight.shape[0]
    half = tok_count // HALVES
    pair = pl.BlockSpec((key_count, half, width), lambda i, s: (0, i, 0))
    return pl.pallas_call(
        functools.partial(cot_kernel, len(sums), model_width),
        grid_spec=pltpu.PrefetchScalarGridSpec(
            num_scalar_prefetch=1,
            grid=(HALVES,),
            in_specs=[pl.BlockSpec((4 * key_count, half), lambda i, s: (0, i))] * len(sums)
            + [pair] * 3
            + [
                pl.BlockSpec((key_count, width, width), lambda i, s: (0, s[0], 0)),
                pl.BlockSpec((width, width), lambda i, s: (s[0], 0)),
            ],
            out_specs=[
                pl.BlockSpec((half, (key_count + 1) * width), lambda i, s: (i, 0)),
                pl.BlockSpec((half, width), lambda i, s: (i, 0)),
            ],
        ),
        out_shape=[
            jax.ShapeDtypeStruct((tok_count, (key_count + 1) * width), BF16),
            jax.ShapeDtypeStruct((tok_count, width), BF16),
        ],
        compiler_params=params(),
        cost_estimate=cost(
            tok_count * width * width * (key_count + 1), 14 * tok_count * width * (key_count + 1)
        ),
        name="cotangents",
    )(shard, *sums, vals, states, grads, key_weight, value_weight)


def back_kernel(shard_ref, joined_ref, key_ref, value_ref, term_ref):
    key_count, width, _ = key_ref.shape
    cots = [joined_ref[:, j * width : (j + 1) * width] for j in range(key_count + 1)]
    term_ref[...] = back_term(cots, key_ref, value_ref).astype(BF16)


def back(shards, joined, key_weight, value_weight):
    count = shards.shape[0]
    key_count, _, width = key_weight.shape
    tok_count = joined.shape[0]
    return pl.pallas_call(
        back_kernel,
        grid_spec=pltpu.PrefetchScalarGridSpec(
            num_scalar_prefetch=1,
            grid=(count,),
            in_specs=[
                pl.BlockSpec(joined.shape, lambda i, s: (0, 0)),
                pl.BlockSpec((key_count, width, width), lambda i, s: (0, s[i], 0)),
                pl.BlockSpec((width, width), lambda i, s: (s[i], 0)),
            ],
            out_specs=pl.BlockSpec((None, tok_count, width), lambda i, s: (i, 0, 0)),
        ),
        out_shape=jax.ShapeDtypeStruct((count, tok_count, width), BF16),
        compiler_params=params(),
        cost_estimate=cost(
            count * tok_count * width * width * (key_count + 1),
            count * 10 * tok_count * width * (key_count + 1),
        ),
        name="back",
    )(shards, joined, key_weight, value_weight)


def outer_kernel(block_ref, turned_ref, joined_ref, *refs):
    product = jnp.dot(turned_ref[...], joined_ref[...], preferred_element_type=F32)
    if len(refs) == 1:
        refs[0][...] = product.astype(BF16)
        return
    arrived_ref, first_ref, second_ref = refs
    product = product + arrived_ref[...].astype(F32)
    top = first_ref.shape[0]
    first_ref[...] = product[:top].astype(BF16)
    second_ref[...] = product[top:].astype(BF16)


def outer(block, rows, turned, joined, arrived=None):
    tok_count, columns = joined.shape
    whole = lambda r: pl.BlockSpec((r, columns), lambda i, s: (0, 0))
    in_specs = [pl.BlockSpec((rows, tok_count), lambda i, s: (s[0], 0)), whole(tok_count)]
    args = [block, turned, joined]
    if arrived is None:
        sizes = [rows]
    else:
        in_specs.append(whole(rows))
        args.append(arrived)
        sizes = [rows // 2, rows - rows // 2]
    return pl.pallas_call(
        outer_kernel,
        grid_spec=pltpu.PrefetchScalarGridSpec(
            num_scalar_prefetch=1, grid=(1,), in_specs=in_specs, out_specs=[whole(r) for r in sizes]
        ),
        out_shape=[jax.ShapeDtypeStruct((r, columns), BF16) for r in sizes],
        compiler_params=params(),
        cost_estimate=cost(
            rows * tok_count * columns, 2 * (rows * tok_count + (tok_count + rows) * columns)
        ),
        name="outer" if arrived is None else "outer_add",
    )(*args)


def halve(blocks, bits, axis):
    mine = [blocks[0]]
    for bit in bits:
        far = sorted((rel for rel in blocks if rel & bit), reverse=True)
        arrived = {rel: swap_over(axis, bit, blocks[rel]) for rel in far}
        mine.append(arrived[bit])
        blocks = {
            rel: (blocks[rel].astype(F32) + arrived[rel ^ bit].astype(F32)).astype(BF16)
            if rel
            else None
            for rel in blocks
            if not rel & bit
        }
    return sum(part.astype(F32) for part in mine)


def on_device(
    retrieved,
    branch_states,
    out_grad,
    key_weight,
    value_weight,
    key_grad_acc,
    value_grad_acc,
    row_index,
    row_tier,
    adam_mean,
    adam_second,
):
    tok_count, key_count, width = branch_states.shape
    groups = lax.axis_size("group")
    shards = lax.axis_size("tensor")
    model_width = width * shards
    owned_rows = adam_mean.shape[0]
    half = tok_count // HALVES
    me = lax.axis_index("group")
    place_z = ring_place(lax.axis_index("tensor"), shards)
    one = lambda x: jnp.reshape(x, (1,)).astype(jnp.int32)

    parts = []
    for h in range(HALVES):
        source = retrieved[h * half : (h + 1) * half]
        if parts:
            source, _ = lax.optimization_barrier((source, parts[0]))
        parts.append(jnp.sum(source.astype(F32), axis=1).astype(BF16))
    states = jnp.transpose(branch_states, (1, 0, 2))
    grads = jnp.transpose(out_grad, (1, 0, 2))
    carry = None
    for step in range(shards):
        shard = one(ring_device((place_z - step) % shards, shards))
        extra = (states, grads) if step == shards - 1 else None
        following = (
            [ring_pass(part, "tensor") for part in parts] if step < shards - 1 else None
        )
        carry = forward(shard, parts, key_weight, value_weight, carry, extra)
        parts = following
    vals, turned, sums = carry
    sums = [sums] + others_over("tensor", sums)

    ahead = [ring_device((place_z + step) % shards, shards) for step in range(shards)]
    joined, term = cotangents(
        one(ahead[-1]), sums, vals, states, grads, key_weight, value_weight
    )
    passing = ring_pass(term, "tensor")
    terms = back(jnp.stack(ahead[-2::-1]).astype(jnp.int32), joined, key_weight, value_weight)

    shard_rows = model_width // groups
    order = sorted(range(0, groups, 2), key=lambda rel: (-bin(rel).count("1"), rel))
    sent = {
        rel: swap_over(
            "group", 1, outer(one(me ^ (rel + 1)), shard_rows, turned, joined)[0]
        )
        for rel in order
    }
    near = {
        rel: outer(one(me ^ rel), shard_rows, turned, joined, sent[rel]) for rel in order
    }
    bits = []
    bit = 2
    while bit < groups:
        bits.append(bit)
        bit *= 2
    weight_sum = jnp.concatenate(
        [
            halve({rel: near[rel][0] for rel in order}, bits, "group"),
            halve({rel: near[rel][1] for rel in order}, bits[::-1], "group"),
        ],
        axis=0,
    )
    key_grad = key_grad_acc + jnp.stack(
        [weight_sum[:, j * width : (j + 1) * width] for j in range(key_count)]
    )
    value_grad = value_grad_acc + weight_sum[:, key_count * width :]

    for step in range(shards - 1):
        total = passing.astype(F32) + terms[step].astype(F32)
        if step < shards - 2:
            passing = ring_pass(total.astype(BF16), "tensor")
    memory_cot = total.astype(BF16)

    routed, _ = lax.optimization_barrier((row_index, joined))
    flat_rows = routed.reshape(-1)
    owner_idx = flat_rows // owned_rows
    local_row = flat_rows - owner_idx * owned_rows
    owner_marks = (owner_idx[:, None] == jnp.arange(groups, dtype=jnp.int32)[None, :]).astype(
        jnp.int32
    )
    slot_place = jnp.sum(jnp.cumsum(owner_marks, axis=0) * owner_marks, axis=1) - 1
    slot_index = (owner_idx * CAP + slot_place).reshape(row_index.shape)
    local_row = local_row.reshape(row_index.shape)
    slots = lax.broadcasted_iota(jnp.int32, (groups * CAP, tok_count), 0)
    marks = [slots == slot_index[:, n][None, :] for n in range(row_index.shape[1])]
    pick = sum(mark.astype(BF16) for mark in marks)
    slot_row = sum(
        jnp.sum(jnp.where(mark, local_row[:, n][None, :] + 1, 0), axis=1)
        for n, mark in enumerate(marks)
    )
    incoming_rows = lax.all_to_all(
        slot_row.reshape(groups, CAP), "group", split_axis=0, concat_axis=0, tiled=True
    ).reshape(-1)
    place = (
        lax.broadcasted_iota(jnp.int32, (owned_rows, groups * CAP), 0) + 1 == incoming_rows[None, :]
    ).astype(BF16)

    outgoing = jnp.dot(pick, memory_cot, preferred_element_type=F32).astype(BF16)
    incoming = lax.all_to_all(
        outgoing.reshape(groups, CAP, width), "group", split_axis=0, concat_axis=0, tiled=True
    ).reshape(groups * CAP, width)
    row_grad = jnp.dot(place, incoming, preferred_element_type=F32)
    row_part = jnp.sum(row_grad * row_grad, axis=1)
    row_sum = row_part + sum(others_over("tensor", row_part))
    is_hot = (row_tier == 1)[:, None]
    mean_hot = 0.9 * adam_mean + 0.1 * row_grad
    second_hot = 0.95 * adam_second + 0.05 * row_grad * row_grad
    step_hot = mean_hot / FIRST_BIAS / (jnp.sqrt(second_hot / SECOND_BIAS) + EPS_ADAM)
    step_cold = row_grad * lax.rsqrt(row_sum / model_width + EPS_NORM)[:, None]
    new_mean = jnp.where(is_hot, mean_hot, adam_mean)
    new_second = jnp.where(is_hot, second_hot, adam_second)
    row_step = jnp.where(is_hot, step_hot, step_cold)
    return (key_grad, value_grad, new_mean, new_second, row_step)


def solution(mesh):
    return jax.shard_map(
        on_device,
        mesh=mesh,
        in_specs=(
            P("group", None, "tensor"),
            P("group", None, "tensor"),
            P("group", None, "tensor"),
            P(None, None, "tensor"),
            P(None, "tensor"),
            P(None, "group", "tensor"),
            P("group", "tensor"),
            P("group", None),
            P("group"),
            P("group", "tensor"),
            P("group", "tensor"),
        ),
        out_specs=(
            P(None, "group", "tensor"),
            P("group", "tensor"),
            P("group", "tensor"),
            P("group", "tensor"),
            P("group", "tensor"),
        ),
        check_vma=False,
    )
```

```python
import functools

import jax
import jax.numpy as jnp
import numpy as np
from jax import lax
from jax.experimental import pallas as pl
from jax.experimental.pallas import tpu as pltpu
from jax.sharding import PartitionSpec as P

CAP = 128
SCALE = 10
HALVES = 2
VMEM_BYTES = 20 * 1024 * 1024


EPS_NORM = 1e-06
EPS_ADAM = 1e-08
FIRST_BIAS = 1.0 - 0.9**10
SECOND_BIAS = 1.0 - 0.95**10

F32, BF16 = jnp.float32, jnp.bfloat16


VMEM = pl.BlockSpec(memory_space=pltpu.VMEM)
SMEM = pl.BlockSpec(memory_space=pltpu.SMEM)
ANY = pl.BlockSpec(memory_space=pl.ANY)
NT = (((1,), (1,)), ((), ()))


def call(kernel, name, in_specs, out_shape, args, macs=0, scratch=(), out_specs=None):
    return pl.pallas_call(
        kernel,
        in_specs=in_specs,
        out_specs=out_specs or [VMEM] * len(out_shape),
        out_shape=out_shape,
        scratch_shapes=scratch,
        compiler_params=pltpu.CompilerParams(vmem_limit_bytes=VMEM_BYTES),
        cost_estimate=pl.CostEstimate(flops=macs // SCALE, bytes_accessed=0, transcendentals=0),
        name=name,
    )(*args)


def ring_order(size):
    return list(range(0, size, 2)) + list(range(1, size, 2))[::-1]


def ring_pass(part, axis):
    size = lax.axis_size(axis)
    order = ring_order(size)
    return lax.ppermute(part, axis, [(order[i], order[(i + 1) % size]) for i in range(size)])


def others_over(axis, part):
    size = lax.axis_size(axis)
    return [
        lax.ppermute(part, axis, [(i, (i + step) % size) for i in range(size)])
        for step in range(1, size)
    ]


def swap_over(axis, bit, part):
    size = lax.axis_size(axis)
    return lax.ppermute(part, axis, [(i, i ^ bit) for i in range(size)])


def weight_rows(ref, rows, j, width):
    if len(ref.shape) == 2:
        return ref[rows, j * width : (j + 1) * width]
    return ref[j, rows]


def join_kernel(after, key_ref, value_ref, *refs):
    out_ref, sems = refs[after:]
    key_count, _, width = key_ref.shape
    copies = []
    for j in range(key_count + 1):
        source = key_ref.at[j] if j < key_count else value_ref
        flat = len(out_ref.shape) == 2
        target = out_ref.at[:, pl.ds(j * width, width)] if flat else out_ref.at[j]
        copies.append(pltpu.make_async_copy(source, target, sems.at[j]))
        copies[-1].start()
    for copy in copies:
        copy.wait()


def join_weights(key_weight, value_weight, after):
    key_count, model_width, width = key_weight.shape
    flat = width % 128 == 0
    shape = (model_width, (key_count + 1) * width) if flat else (key_count + 1, model_width, width)
    return call(
        functools.partial(join_kernel, len(after)),
        "join_weights",
        [ANY] * (2 + len(after)),
        [jax.ShapeDtypeStruct(shape, BF16)],
        [key_weight, value_weight, *after],
        scratch=[pltpu.SemaphoreType.DMA((key_count + 1,))],
    )[0]


def forward_kernel(h, steps, table_ref, *refs):
    parts, refs = refs[:steps], refs[steps:]
    weight_ref, state_ref, grad_ref, *before = refs[: 3 + (h > 0)]
    val_ref, turned_ref, sum_ref, memory_ref = refs[3 + (h > 0) :]
    key_count, half, width = val_ref.shape
    rows = slice(h * half, (h + 1) * half)
    places = []
    for step in range(steps):
        place = pl.multiple_of(table_ref[step] * width, width)
        places.append(place)
        turned_ref[pl.ds(place, width), :] = parts[step][...].T
        if width % 128 == 0:
            memory_ref[:, pl.ds(place, width)] = parts[step][...]

    def product(j):
        if width % 128 == 0:
            weight = weight_rows(weight_ref, slice(None), j, width)
            return jnp.dot(memory_ref[...], weight, preferred_element_type=F32)
        return sum(
            jnp.dot(
                parts[step][...],
                weight_rows(weight_ref, pl.ds(places[step], width), j, width),
                preferred_element_type=F32,
            )
            for step in range(steps)
        )

    row_sum = lambda x: jnp.sum(x, axis=1, keepdims=True)
    sums = [None] * (4 * key_count)
    for j in range(key_count):
        val = product(j)
        val_ref[j] = val
        state = state_ref[j, rows].astype(F32)
        sums[j] = row_sum(state * state)
        sums[key_count + j] = row_sum(val * val)
        sums[2 * key_count + j] = row_sum(state * val)
    val = product(key_count)
    for j in range(key_count):
        sums[3 * key_count + j] = row_sum(grad_ref[j, rows].astype(F32) * val)
    lane = lax.broadcasted_iota(jnp.int32, (half, 128), 1)
    table = jnp.zeros((half, 128), F32)
    for i, s in enumerate(sums):
        table = jnp.where(lane == i, s, table)
    if h:
        sum_ref[:, : h * half] = before[0][...]
    sum_ref[:, rows] = table.T[: 4 * key_count]


def forward(h, table, parts, weights, states, grads, before):
    half, width = parts[0].shape
    key_count = states.shape[0]
    model_width = weights.shape[-2]
    return call(
        functools.partial(forward_kernel, h, len(parts)),
        "forward",
        [SMEM] + [VMEM] * (len(parts) + 3 + len(before)),
        [
            jax.ShapeDtypeStruct((key_count, half, width), F32),
            jax.ShapeDtypeStruct((model_width, half), BF16),
            jax.ShapeDtypeStruct((4 * key_count, (h + 1) * half), F32),
        ],
        [table, *parts, weights, states, grads, *before],
        macs=half * model_width * width * (key_count + 1),
        scratch=[pltpu.VMEM((half, model_width), BF16)],
    )


def cot_kernel(sums_count, model_width, *refs):
    sum_refs, refs = refs[:sums_count], refs[sums_count:]
    val_refs, (state_ref, grad_ref, joined_ref) = refs[:HALVES], refs[HALVES:]
    key_count, half, width = val_refs[0].shape
    total = sum_refs[0][...]
    for ref in sum_refs[1:]:
        total = total + ref[...]
    root_width = jnp.sqrt(F32(model_width))
    state_sum, key_sum, cross_dot, out_dot = (
        total[i * key_count : (i + 1) * key_count] for i in range(4)
    )
    state_rs = lax.rsqrt(state_sum / model_width + EPS_NORM)
    key_rs = lax.rsqrt(key_sum / model_width + EPS_NORM)
    scores = cross_dot * state_rs * key_rs / root_width
    gate_val = 1.0 / (1.0 + jnp.exp(-scores))
    dscore = out_dot * gate_val * (1.0 - gate_val)
    lead = key_rs * dscore / root_width
    slope = key_rs * scores / root_width
    factors = jnp.concatenate([lead, state_rs, slope, gate_val], axis=0)
    filler = jnp.zeros((128 - 4 * key_count, half), F32)
    for h in range(HALVES):
        rows = slice(h * half, (h + 1) * half)
        table = jnp.concatenate([factors[:, rows], filler], axis=0).T
        column = lambda kind, j: table[:, kind * key_count + j : kind * key_count + j + 1]
        value_cot = None
        for j in range(key_count):
            state = state_ref[j, rows].astype(F32)
            inner = state * column(1, j) - val_refs[h][j] * column(2, j)
            joined_ref[rows, j * width : (j + 1) * width] = (column(0, j) * inner).astype(BF16)
            gated = column(3, j) * grad_ref[j, rows].astype(F32)
            value_cot = gated if value_cot is None else value_cot + gated
        joined_ref[rows, key_count * width :] = value_cot.astype(BF16)


def cotangents(sums, vals, states, grads, model_width):
    key_count, tok_count, width = states.shape
    return call(
        functools.partial(cot_kernel, len(sums), model_width),
        "cotangents",
        [VMEM] * (len(sums) + len(vals) + 2),
        [jax.ShapeDtypeStruct((tok_count, (key_count + 1) * width), BF16)],
        [*sums, *vals, states, grads],
        macs=tok_count * width,
    )[0]


def back_kernel(step, after, table_ref, joined_ref, weight_ref, *refs):
    refs = refs[after:]
    width = sum(ref.shape[1] for ref in refs)
    place = pl.multiple_of(table_ref[step] * width, width)
    rows = pl.ds(place, width)
    if len(weight_ref.shape) == 2:
        term = lax.dot_general(
            joined_ref[...], weight_ref[rows, :], NT, preferred_element_type=F32
        )
    else:
        term = sum(
            lax.dot_general(
                joined_ref[:, j * width : (j + 1) * width],
                weight_ref[j, rows],
                NT,
                preferred_element_type=F32,
            )
            for j in range(weight_ref.shape[0])
        )
    start = 0
    for ref in refs:
        ref[...] = term[:, start : start + ref.shape[1]].astype(BF16)
        start += ref.shape[1]


def back(step, table, joined, weights, cuts, after=()):
    tok_count, columns = joined.shape
    return call(
        functools.partial(back_kernel, step, len(after)),
        "back",
        [SMEM] + [VMEM] * 2 + [ANY] * len(after),
        [jax.ShapeDtypeStruct((tok_count, cut), BF16) for cut in cuts],
        [table, joined, weights, *after],
        macs=tok_count * columns * sum(cuts),
    )


def outer_kernel(entry, after, plan_ref, joined_ref, other_joined_ref, *refs):
    turned, others, refs = refs[:HALVES], refs[HALVES : 2 * HALVES], refs[2 * HALVES + after :]
    rows = sum(ref.shape[0] for ref in refs)
    place = pl.multiple_of(plan_ref[entry] * rows, rows)
    block = lambda halves: jnp.concatenate([ref[pl.ds(place, rows), :] for ref in halves], axis=1)
    product = jnp.dot(block(turned), joined_ref[...], preferred_element_type=F32)
    product = product + jnp.dot(block(others), other_joined_ref[...], preferred_element_type=F32)
    start = 0
    for ref in refs:
        ref[...] = product[start : start + ref.shape[0]].astype(BF16)
        start += ref.shape[0]


def outer(rel, skip, plan, rows, joined, other_joined, turned, other_turned, after=()):
    tok_count, columns = joined.shape
    return call(
        functools.partial(outer_kernel, skip + rel, len(after)),
        "outer",
        [SMEM] + [VMEM] * (2 + 2 * HALVES) + [ANY] * len(after),
        [jax.ShapeDtypeStruct((r, columns), BF16) for r in (rows // 2, rows - rows // 2)],
        [plan, joined, other_joined, *turned, *other_turned, *after],
        macs=2 * rows * tok_count * columns,
    )


def sum_kernel(*refs):
    total = refs[0][...].astype(F32)
    for ref in refs[1:-1]:
        total = total + ref[...].astype(F32)
    refs[-1][...] = total.astype(refs[-1].dtype)


def add(*parts):
    return call(
        sum_kernel,
        "add",
        [VMEM] * len(parts),
        [jax.ShapeDtypeStruct(parts[0].shape, BF16)],
        parts,
        macs=parts[0].size,
    )[0]


def pick_kernel(slot_ref, passing_ref, term_ref, out_ref):
    total = (passing_ref[...].astype(F32) + term_ref[...].astype(F32)).astype(BF16)
    slots = lax.broadcasted_iota(jnp.int32, (out_ref.shape[0], total.shape[0]), 0)
    pick = sum(
        (slots == slot_ref[n : n + 1, :]).astype(F32) for n in range(slot_ref.shape[0])
    ).astype(BF16)
    out_ref[...] = jnp.dot(pick, total, preferred_element_type=F32).astype(BF16)


def pick_rows(slot_index, passing, term, slot_count):
    tok_count, cut = passing.shape
    return call(
        pick_kernel,
        "pick_rows",
        [VMEM] * 3,
        [jax.ShapeDtypeStruct((slot_count, cut), BF16)],
        [slot_index, passing, term],
        macs=slot_count * tok_count * cut,
    )[0]


def place_kernel(row_ref, incoming_ref, grad_ref, sum_ref):
    rows = lax.broadcasted_iota(jnp.int32, (grad_ref.shape[0], row_ref.shape[1]), 0) + 1
    place = (rows == row_ref[...]).astype(F32).astype(BF16)
    grad = jnp.dot(place, incoming_ref[...], preferred_element_type=F32)
    grad_ref[...] = grad
    sum_ref[...] = jnp.sum(grad * grad, axis=1, keepdims=True)


def place_rows(incoming_rows, incoming, owned_rows):
    slot_count, cut = incoming.shape
    return call(
        place_kernel,
        "place_rows",
        [VMEM] * 2,
        [
            jax.ShapeDtypeStruct((owned_rows, cut), F32),
            jax.ShapeDtypeStruct((owned_rows, 1), F32),
        ],
        [incoming_rows, incoming],
        macs=slot_count * owned_rows * cut,
    )


def halve(blocks, bits, axis):
    mine = [blocks[0]]
    for bit in bits:
        far = sorted((rel for rel in blocks if rel & bit), reverse=True)
        arrived = {rel: swap_over(axis, bit, blocks[rel]) for rel in far}
        mine.append(arrived[bit])
        blocks = {
            rel: add(blocks[rel], arrived[rel ^ bit]) if rel else None
            for rel in blocks
            if not rel & bit
        }
    return sum(part.astype(F32) for part in mine)


def on_device(
    retrieved,
    branch_states,
    out_grad,
    key_weight,
    value_weight,
    key_grad_acc,
    value_grad_acc,
    row_index,
    row_tier,
    adam_mean,
    adam_second,
):
    tok_count, key_count, width = branch_states.shape
    groups = lax.axis_size("group")
    shards = lax.axis_size("tensor")
    model_width = width * shards
    owned_rows = adam_mean.shape[0]
    half = tok_count // HALVES
    me = lax.axis_index("group")
    line = lax.axis_index("tensor")
    order = ring_order(shards)
    behind, ahead = np.zeros((shards, shards), np.int32), np.zeros((shards, shards), np.int32)
    for spot, device in enumerate(order):
        for step in range(shards):
            behind[device, step] = order[(spot - step) % shards]
            ahead[device, step] = order[(spot - 1 - step) % shards]
    plan = jnp.concatenate(
        [
            lax.dynamic_index_in_dim(jnp.asarray(np.concatenate([behind, ahead], 1)), line, 0, False),
            jnp.arange(groups, dtype=jnp.int32) ^ me,
        ]
    )

    by_row = lambda x: lax.optimization_barrier(jnp.transpose(x, (1, 0, 2)))
    chains = []
    for h in range(HALVES):
        rows = by_row(retrieved[h * half : (h + 1) * half])
        chains.append([jnp.sum(rows.astype(F32), axis=0).astype(BF16)])
    for step in range(shards - 1):
        for chain in chains:
            chain.append(ring_pass(chain[-1], "tensor"))
    states, grads = by_row(branch_states), by_row(out_grad)

    routed, _ = lax.optimization_barrier((row_index.T, chains[0][1]))
    owner_idx = routed // owned_rows
    local_row = routed - owner_idx * owned_rows
    flat_owner = owner_idx.T.reshape(-1)
    owner_marks = (flat_owner[:, None] == jnp.arange(groups, dtype=jnp.int32)[None, :]).astype(
        jnp.int32
    )
    slot_place = jnp.sum(jnp.cumsum(owner_marks, axis=0) * owner_marks, axis=1) - 1
    slot_index = owner_idx * CAP + slot_place.reshape(row_index.shape).T
    slots = lax.broadcasted_iota(jnp.int32, (groups * CAP, tok_count), 0)
    slot_row = sum(
        jnp.sum(
            jnp.where(slots == slot_index[n][None, :], local_row[n][None, :] + 1, 0), axis=1
        )
        for n in range(row_index.shape[1])
    )
    incoming_rows = lax.all_to_all(
        slot_row.reshape(groups, CAP), "group", split_axis=0, concat_axis=0, tiled=True
    ).reshape(1, -1)

    weights = join_weights(
        key_weight, value_weight, (incoming_rows, slot_index, states, grads, plan)
    )
    vals, turned, sums = [], [], []
    for h, chain in enumerate(chains):
        val, turn, sums_here = forward(h, plan, chain, weights, states, grads, sums)
        vals.append(val)
        turned.append(turn)
        sums = [sums_here]
    sums += others_over("tensor", sums[0])
    other_turned = [swap_over("group", 1, turn) for turn in turned]

    lanes = -(-width // 256) * 128
    cuts = [lanes, width - lanes] if width > lanes else [width]
    joined = cotangents(sums, vals, states, grads, model_width)
    other_joined = swap_over("group", 1, joined)
    passing = [ring_pass(part, "tensor") for part in back(shards, plan, joined, weights, cuts)]

    shard_rows = model_width // groups
    order = sorted(range(0, groups, 2), key=lambda rel: (-bin(rel).count("1"), rel))
    near, terms, last = {}, [], ()
    for k, rel in enumerate(order):
        near[rel] = outer(
            rel, 2 * shards, plan, shard_rows, joined, other_joined, turned, other_turned, last
        )
        last = near[rel][:1]
        if k and len(terms) < shards - 1:
            terms.append(back(shards + len(terms) + 1, plan, joined, weights, cuts, last))
            last = terms[-1][:1]
    while len(terms) < shards - 1:
        terms.append(back(shards + len(terms) + 1, plan, joined, weights, cuts, last))
        last = terms[-1][:1]
    bits = []
    bit = 2
    while bit < groups:
        bits.append(bit)
        bit *= 2
    weight_sum = jnp.concatenate(
        [
            halve({rel: near[rel][0] for rel in order}, bits, "group"),
            halve({rel: near[rel][1] for rel in order}, bits[::-1], "group"),
        ],
        axis=0,
    )
    key_grad = key_grad_acc + jnp.stack(
        [weight_sum[:, j * width : (j + 1) * width] for j in range(key_count)]
    )
    value_grad = value_grad_acc + weight_sum[:, key_count * width :]

    for step in range(shards - 2):
        passing = [
            ring_pass(add(part, term), "tensor") for part, term in zip(passing, terms[step])
        ]
    row_grads, row_parts = [], []
    for part, term in zip(passing, terms[-1]):
        outgoing = pick_rows(slot_index, part, term, groups * CAP)
        incoming = lax.all_to_all(
            outgoing.reshape(groups, CAP, -1), "group", split_axis=0, concat_axis=0, tiled=True
        ).reshape(groups * CAP, -1)
        grad, part_sum = place_rows(incoming_rows, incoming, owned_rows)
        row_grads.append(grad)
        row_parts.append(part_sum[:, 0])
    row_grad = jnp.concatenate(row_grads, axis=1)
    row_part = sum(row_parts)
    row_sum = row_part + sum(others_over("tensor", row_part))
    is_hot = (row_tier == 1)[:, None]
    mean_hot = 0.9 * adam_mean + 0.1 * row_grad
    second_hot = 0.95 * adam_second + 0.05 * row_grad * row_grad
    step_hot = mean_hot / FIRST_BIAS / (jnp.sqrt(second_hot / SECOND_BIAS) + EPS_ADAM)
    step_cold = row_grad * lax.rsqrt(row_sum / model_width + EPS_NORM)[:, None]
    new_mean = jnp.where(is_hot, mean_hot, adam_mean)
    new_second = jnp.where(is_hot, second_hot, adam_second)
    row_step = jnp.where(is_hot, step_hot, step_cold)
    return (key_grad, value_grad, new_mean, new_second, row_step)


def solution(mesh):
    return jax.shard_map(
        on_device,
        mesh=mesh,
        in_specs=(
            P("group", None, "tensor"),
            P("group", None, "tensor"),
            P("group", None, "tensor"),
            P(None, None, "tensor"),
            P(None, "tensor"),
            P(None, "group", "tensor"),
            P("group", "tensor"),
            P("group", None),
            P("group"),
            P("group", "tensor"),
            P("group", "tensor"),
        ),
        out_specs=(
            P(None, "group", "tensor"),
            P("group", "tensor"),
            P("group", "tensor"),
            P("group", "tensor"),
            P("group", "tensor"),
        ),
        check_vma=False,
    )
```

```python
import functools

import jax
import jax.numpy as jnp
import numpy as np
from jax import lax
from jax.experimental import pallas as pl
from jax.experimental.pallas import tpu as pltpu
from jax.sharding import PartitionSpec as P

CAP = 128
SCALE = 10
HALVES = 2
VMEM_BYTES = 20 * 1024 * 1024


EPS_NORM = 1e-06
EPS_ADAM = 1e-08
FIRST_BIAS = 1.0 - 0.9**10
SECOND_BIAS = 1.0 - 0.95**10

F32, BF16 = jnp.float32, jnp.bfloat16


VMEM = pl.BlockSpec(memory_space=pltpu.VMEM)
SMEM = pl.BlockSpec(memory_space=pltpu.SMEM)
ANY = pl.BlockSpec(memory_space=pl.ANY)
NT = (((1,), (1,)), ((), ()))


def call(kernel, name, in_specs, out_shape, args, macs=0, scratch=(), aliases=None, after=()):
    count = len(args)

    def body(*refs):
        kernel(*refs[:count], *refs[count + len(after) :])

    return pl.pallas_call(
        body,
        in_specs=in_specs + [ANY] * len(after),
        out_specs=[VMEM] * len(out_shape),
        out_shape=out_shape,
        scratch_shapes=scratch,
        input_output_aliases=aliases or {},
        compiler_params=pltpu.CompilerParams(vmem_limit_bytes=VMEM_BYTES),
        cost_estimate=pl.CostEstimate(flops=macs // SCALE, bytes_accessed=0, transcendentals=0),
        name=name,
    )(*args, *after)


def ring_order(size):
    return list(range(0, size, 2)) + list(range(1, size, 2))[::-1]


def ring_pass(part, axis):
    size = lax.axis_size(axis)
    order = ring_order(size)
    return lax.ppermute(part, axis, [(order[i], order[(i + 1) % size]) for i in range(size)])


def others_over(axis, part):
    size = lax.axis_size(axis)
    return [
        lax.ppermute(part, axis, [(i, i ^ step) for i in range(size)])
        for step in range(1, size)
    ]


def swap_over(axis, bit, part):
    size = lax.axis_size(axis)
    return lax.ppermute(part, axis, [(i, i ^ bit) for i in range(size)])


def after_kernel(*refs):
    del refs


def after(x, *others):
    return pl.pallas_call(
        after_kernel,
        in_specs=[ANY] * (1 + len(others)),
        out_specs=ANY,
        out_shape=jax.ShapeDtypeStruct(x.shape, x.dtype),
        input_output_aliases={0: 0},
        compiler_params=pltpu.CompilerParams(vmem_limit_bytes=1024 * 1024),
        name="after",
    )(x, *others)


def weight_block(ref, rows, j, width):
    if len(ref.shape) == 2:
        return ref[rows, j * width : (j + 1) * width]
    return ref[j, rows]


def join_kernel(plan_ref, key_ref, value_ref, out_ref, sems):
    key_count, model_width, width = key_ref.shape
    copies = []
    for step in range(model_width // width):
        source_rows = pl.ds(pl.multiple_of(plan_ref[step] * width, width), width)
        rows = pl.ds(step * width, width)
        for j in range(key_count + 1):
            source = key_ref.at[j, source_rows, :] if j < key_count else value_ref.at[source_rows, :]
            if len(out_ref.shape) == 2:
                target = out_ref.at[rows, pl.ds(j * width, width)]
            else:
                target = out_ref.at[j, rows, :]
            copies.append(pltpu.make_async_copy(source, target, sems.at[step, j]))
            copies[-1].start()
    for copy in copies:
        copy.wait()


def join_weights(plan, key_weight, value_weight, after):
    key_count, model_width, width = key_weight.shape
    flat = width % 128 == 0
    shape = (model_width, (key_count + 1) * width) if flat else (key_count + 1, model_width, width)
    return call(
        join_kernel,
        "join_weights",
        [SMEM] + [ANY] * 2,
        [jax.ShapeDtypeStruct(shape, BF16)],
        [plan, key_weight, value_weight],
        scratch=[pltpu.SemaphoreType.DMA((model_width // width, key_count + 1))],
        after=after,
    )[0]


def partial_products(parts, weight_ref, first, j):
    width = parts[0].shape[1]
    if len(weight_ref.shape) == 2:
        rows = slice(first * width, (first + len(parts)) * width)
        whole = jnp.concatenate(parts, axis=1) if len(parts) > 1 else parts[0]
        weight = weight_block(weight_ref, rows, j, width)
        return jnp.dot(whole, weight, preferred_element_type=F32)
    return sum(
        jnp.dot(
            part,
            weight_block(weight_ref, slice((first + k) * width, (first + k + 1) * width), j, width),
            preferred_element_type=F32,
        )
        for k, part in enumerate(parts)
    )


def early_kernel(steps, plan_ref, weight_ref, *refs):
    *part_refs, acc_ref, turned_ref = refs
    width = acc_ref.shape[2]
    parts = [
        jnp.concatenate([part_refs[h * steps + step][...] for h in range(HALVES)], axis=0)
        for step in range(steps)
    ]
    for j in range(acc_ref.shape[0]):
        acc_ref[j] = partial_products(parts, weight_ref, 0, j)
    for step in range(steps):
        turned_ref[pl.ds(pl.multiple_of(plan_ref[step] * width, width), width), :] = parts[step].T


def forward_early(plan, weights, chains, key_count):
    steps = len(chains[0])
    half, width = chains[0][0].shape
    tok_count = half * HALVES
    return call(
        functools.partial(early_kernel, steps),
        "forward_early",
        [SMEM] + [VMEM] * (1 + HALVES * steps),
        [
            jax.ShapeDtypeStruct((key_count + 1, tok_count, width), F32),
            jax.ShapeDtypeStruct((weights.shape[-2], tok_count), BF16),
        ],
        [plan, weights] + [part for chain in chains for part in chain],
        macs=tok_count * steps * width * width * (key_count + 1),
    )


def late_kernel(step, plan_ref, weight_ref, *refs):
    part_refs, refs = refs[:HALVES], refs[HALVES:]
    acc_ref, _, state_ref, grad_ref, val_ref, turned_ref, sum_ref = refs
    key_count, tok_count, width = state_ref.shape
    part = jnp.concatenate([ref[...] for ref in part_refs], axis=0)
    row_sum = lambda x: jnp.sum(x, axis=1, keepdims=True)
    sums = [None] * (4 * key_count)
    for j in range(key_count + 1):
        val = acc_ref[j] + partial_products([part], weight_ref, step, j)
        if j == key_count:
            for k in range(key_count):
                sums[3 * key_count + k] = row_sum(grad_ref[k].astype(F32) * val)
            continue
        val_ref[j] = val
        state = state_ref[j].astype(F32)
        sums[j] = row_sum(state * state)
        sums[key_count + j] = row_sum(val * val)
        sums[2 * key_count + j] = row_sum(state * val)
    lane = lax.broadcasted_iota(jnp.int32, (tok_count, 128), 1)
    table = jnp.zeros((tok_count, 128), F32)
    for i, s in enumerate(sums):
        table = jnp.where(lane == i, s, table)
    sum_ref[...] = table.T[: 4 * key_count]
    turned_ref[pl.ds(pl.multiple_of(plan_ref[step] * width, width), width), :] = part.T


def forward_late(plan, weights, parts, acc, turned, states, grads):
    key_count, tok_count, width = states.shape
    return call(
        functools.partial(late_kernel, weights.shape[-2] // width - 1),
        "forward_late",
        [SMEM] + [VMEM] * (5 + HALVES),
        [
            jax.ShapeDtypeStruct(acc.shape, F32),
            jax.ShapeDtypeStruct(turned.shape, BF16),
            jax.ShapeDtypeStruct((4 * key_count, tok_count), F32),
        ],
        [plan, weights, *parts, acc, turned, states, grads],
        macs=tok_count * width * width * (key_count + 1),
        aliases={2 + HALVES: 0, 3 + HALVES: 1},
    )


def cot_kernel(sums_count, model_width, *refs):
    sum_refs, refs = refs[:sums_count], refs[sums_count:]
    val_ref, state_ref, grad_ref, joined_ref = refs
    key_count, tok_count, width = state_ref.shape
    half = tok_count // HALVES
    total = sum_refs[0][...]
    for ref in sum_refs[1:]:
        total = total + ref[...]
    root_width = jnp.sqrt(F32(model_width))
    state_sum, key_sum, cross_dot, out_dot = (
        total[i * key_count : (i + 1) * key_count] for i in range(4)
    )
    state_rs = lax.rsqrt(state_sum / model_width + EPS_NORM)
    key_rs = lax.rsqrt(key_sum / model_width + EPS_NORM)
    scores = cross_dot * state_rs * key_rs / root_width
    gate_val = 1.0 / (1.0 + jnp.exp(-scores))
    dscore = out_dot * gate_val * (1.0 - gate_val)
    lead = key_rs * dscore / root_width
    slope = key_rs * scores / root_width
    factors = jnp.concatenate([lead, state_rs, slope, gate_val], axis=0)
    filler = jnp.zeros((128 - 4 * key_count, half), F32)
    for h in range(HALVES):
        rows = slice(h * half, (h + 1) * half)
        table = jnp.concatenate([factors[:, rows], filler], axis=0).T
        column = lambda kind, j: table[:, kind * key_count + j : kind * key_count + j + 1]
        value_cot = None
        for j in range(key_count):
            state = state_ref[j, rows].astype(F32)
            inner = state * column(1, j) - val_ref[j, rows] * column(2, j)
            joined_ref[rows, j * width : (j + 1) * width] = (column(0, j) * inner).astype(BF16)
            gated = column(3, j) * grad_ref[j, rows].astype(F32)
            value_cot = gated if value_cot is None else value_cot + gated
        joined_ref[rows, key_count * width :] = value_cot.astype(BF16)


def cotangents(sums, vals, states, grads, model_width, after):
    key_count, tok_count, width = states.shape
    return call(
        functools.partial(cot_kernel, len(sums), model_width),
        "cotangents",
        [VMEM] * (len(sums) + 3),
        [jax.ShapeDtypeStruct((tok_count, (key_count + 1) * width), BF16)],
        [*sums, vals, states, grads],
        macs=tok_count * width,
        after=after,
    )[0]


def back_kernel(step, joined_ref, weight_ref, *refs):
    width = sum(ref.shape[1] for ref in refs)
    rows = slice(step * width, (step + 1) * width)
    if len(weight_ref.shape) == 2:
        term = lax.dot_general(
            joined_ref[...], weight_ref[rows], NT, preferred_element_type=F32
        )
    else:
        term = sum(
            lax.dot_general(
                joined_ref[:, j * width : (j + 1) * width],
                weight_ref[j, rows],
                NT,
                preferred_element_type=F32,
            )
            for j in range(weight_ref.shape[0])
        )
    start = 0
    for ref in refs:
        ref[...] = term[:, start : start + ref.shape[1]].astype(BF16)
        start += ref.shape[1]


def back(step, joined, weights, cuts, after=()):
    tok_count, columns = joined.shape
    return call(
        functools.partial(back_kernel, step),
        "back",
        [VMEM] * 2,
        [jax.ShapeDtypeStruct((tok_count, cut), BF16) for cut in cuts],
        [joined, weights],
        macs=tok_count * columns * sum(cuts),
        after=after,
    )


def outer_kernel(
    entry, plan_ref, joined_ref, other_joined_ref, turned_ref, other_turned_ref, *refs
):
    rows = sum(ref.shape[0] for ref in refs)
    block = pl.ds(pl.multiple_of(plan_ref[entry] * rows, rows), rows)
    product = jnp.dot(turned_ref[block, :], joined_ref[...], preferred_element_type=F32)
    product = product + jnp.dot(
        other_turned_ref[block, :], other_joined_ref[...], preferred_element_type=F32
    )
    start = 0
    for ref in refs:
        ref[...] = product[start : start + ref.shape[0]].astype(BF16)
        start += ref.shape[0]


def outer(entry, plan, rows, joined, other_joined, turned, other_turned, after=()):
    tok_count, columns = joined.shape
    return call(
        functools.partial(outer_kernel, entry),
        "outer",
        [SMEM] + [VMEM] * 4,
        [jax.ShapeDtypeStruct((r, columns), BF16) for r in (rows // 2, rows - rows // 2)],
        [plan, joined, other_joined, turned, other_turned],
        macs=2 * rows * tok_count * columns,
        after=after,
    )


def route_kernel(owned_rows, row_ref, slot_ref, out_ref):
    grams, tok_count = row_ref.shape
    groups = out_ref.shape[0]
    nt = functools.partial(lax.dot_general, dimension_numbers=NT, preferred_element_type=F32)
    flag = lambda x: x.astype(F32).astype(BF16)
    before = lax.broadcasted_iota(jnp.int32, (tok_count, tok_count), 0)
    before = flag(before <= lax.broadcasted_iota(jnp.int32, (tok_count, tok_count), 1))
    owners = lax.broadcasted_iota(jnp.int32, (groups, tok_count), 0)
    slots = lax.broadcasted_iota(jnp.int32, (groups * CAP, tok_count), 0)
    taken = jnp.zeros((groups, 1), F32)
    held = jnp.zeros((16, groups * CAP), F32)
    for n in range(grams):
        row = row_ref[n : n + 1, :]
        owner = row // owned_rows
        mine = owners == owner
        count = jnp.dot(flag(mine), before, preferred_element_type=F32) + taken
        taken = count[:, tok_count - 1 :]
        place = jnp.sum(jnp.where(mine, count, 0.0), axis=0, keepdims=True).astype(jnp.int32) - 1
        slot = owner * CAP + place
        slot_ref[n : n + 1, :] = slot
        local = row - owner * owned_rows + 1
        digits = jnp.concatenate([local // 128, local % 128], axis=0).astype(F32)
        digits = jnp.concatenate([digits, jnp.zeros((14, tok_count), F32)], axis=0).astype(BF16)
        held = held + nt(digits, flag(slots == slot))
    found = (held[0:1] * 128.0 + held[1:2]).astype(jnp.int32)
    for group in range(groups):
        out_ref[group : group + 1, :] = found[:, group * CAP : (group + 1) * CAP]


def route(rows, owned_rows, groups, after=()):
    return call(
        functools.partial(route_kernel, owned_rows),
        "route",
        [VMEM],
        [
            jax.ShapeDtypeStruct(rows.shape, jnp.int32),
            jax.ShapeDtypeStruct((groups, CAP), jnp.int32),
        ],
        [rows],
        macs=rows.size * rows.shape[1],
        after=after,
    )


def memory_kernel(h, rows_ref, out_ref):
    half = out_ref.shape[0]
    part = slice(h * half, (h + 1) * half)
    total = rows_ref[0, part].astype(F32)
    for n in range(1, rows_ref.shape[0]):
        total = total + rows_ref[n, part].astype(F32)
    out_ref[...] = total.astype(BF16)


def sum_rows(h, rows, after):
    _, tok_count, width = rows.shape
    return call(
        functools.partial(memory_kernel, h),
        "sum_rows",
        [VMEM],
        [jax.ShapeDtypeStruct((tok_count // HALVES, width), BF16)],
        [rows],
        macs=tok_count * width,
        after=after,
    )[0]


def sum_kernel(*refs):
    total = refs[0][...].astype(F32)
    for ref in refs[1:-1]:
        total = total + ref[...].astype(F32)
    refs[-1][...] = total.astype(refs[-1].dtype)


def add(*parts, after=(), dtype=BF16):
    return call(
        sum_kernel,
        "add",
        [VMEM] * len(parts),
        [jax.ShapeDtypeStruct(parts[0].shape, dtype)],
        parts,
        macs=parts[0].size,
        after=after,
    )[0]


def part_kernel(start, whole_ref, part_ref, out_ref):
    whole = whole_ref[:, start : start + part_ref.shape[1]]
    out_ref[...] = (whole.astype(F32) + part_ref[...].astype(F32)).astype(BF16)


def add_part(whole, part, start, after=()):
    return call(
        functools.partial(part_kernel, start),
        "add_part",
        [VMEM] * 2,
        [jax.ShapeDtypeStruct(part.shape, BF16)],
        [whole, part],
        macs=part.size,
        after=after,
    )[0]


def mark_kernel(slot_ref, out_ref):
    slots = lax.broadcasted_iota(jnp.int32, out_ref.shape, 0)
    marks = sum((slots == slot_ref[n : n + 1, :]).astype(F32) for n in range(slot_ref.shape[0]))
    out_ref[...] = marks.astype(BF16)


def mark_slots(slot_index, slot_count, after=()):
    return call(
        mark_kernel,
        "mark_slots",
        [VMEM],
        [jax.ShapeDtypeStruct((slot_count, slot_index.shape[1]), BF16)],
        [slot_index],
        macs=slot_count * slot_index.shape[1],
        after=after,
    )[0]


def pick_kernel(mark_ref, *refs):
    *refs, out_ref = refs
    count = len(refs) // 2
    start = 0
    for passing_ref, term_ref in zip(refs[:count], refs[count:]):
        total = (passing_ref[...].astype(F32) + term_ref[...].astype(F32)).astype(BF16)
        columns = slice(start, start + total.shape[1])
        product = jnp.dot(mark_ref[...], total, preferred_element_type=F32)
        out_ref[:, columns] = product.astype(BF16)
        start += total.shape[1]


def pick_rows(marks, passing, terms, after=()):
    slot_count, tok_count = marks.shape
    width = sum(part.shape[1] for part in passing)
    return call(
        pick_kernel,
        "pick_rows",
        [VMEM] * (1 + 2 * len(passing)),
        [jax.ShapeDtypeStruct((slot_count, width), BF16)],
        [marks, *passing, *terms],
        macs=slot_count * tok_count * width,
        after=after,
    )[0]


def place_kernel(row_ref, incoming_ref, grad_ref, sum_ref):
    rows = lax.broadcasted_iota(jnp.int32, (grad_ref.shape[0], row_ref.shape[1]), 0) + 1
    place = (rows == row_ref[...]).astype(F32).astype(BF16)
    grad = jnp.dot(place, incoming_ref[...], preferred_element_type=F32)
    grad_ref[...] = grad
    sums = jnp.sum(grad * grad, axis=1, keepdims=True)
    sum_ref[...] = jnp.broadcast_to(sums, (sums.shape[0], 128)).T[:1]


def place_rows(incoming_rows, incoming, owned_rows, after=()):
    cut = incoming.shape[1]
    return call(
        place_kernel,
        "place_rows",
        [VMEM] * 2,
        [
            jax.ShapeDtypeStruct((owned_rows, cut), F32),
            jax.ShapeDtypeStruct((1, owned_rows), F32),
        ],
        [incoming_rows, incoming],
        macs=incoming.size * owned_rows,
        after=after,
    )


def adam_kernel(model_width, tier_ref, mean_ref, second_ref, grad_ref, *refs):
    *sum_refs, new_mean_ref, new_second_ref, step_ref = refs
    row_sum = sum_refs[0][...]
    for ref in sum_refs[1:]:
        row_sum = row_sum + ref[...]
    scale = lax.rsqrt(row_sum / model_width + EPS_NORM)
    hot = (tier_ref[...] == 1).astype(F32)
    filler = jnp.zeros((126, scale.shape[1]), F32)
    table = jnp.concatenate([scale, hot, filler], axis=0).T
    is_hot = table[:, 1:2] > 0.5
    grad = grad_ref[...]
    mean_hot = 0.9 * mean_ref[...] + 0.1 * grad
    second_hot = 0.95 * second_ref[...] + 0.05 * grad * grad
    step_hot = mean_hot / FIRST_BIAS / (jnp.sqrt(second_hot / SECOND_BIAS) + EPS_ADAM)
    new_mean_ref[...] = jnp.where(is_hot, mean_hot, mean_ref[...])
    new_second_ref[...] = jnp.where(is_hot, second_hot, second_ref[...])
    step_ref[...] = jnp.where(is_hot, step_hot, grad * table[:, :1])


def adam(model_width, row_tier, adam_mean, adam_second, row_grad, row_sums):
    owned_rows, width = row_grad.shape
    tile = 128 if owned_rows % 128 == 0 else owned_rows
    rows = pl.BlockSpec((tile, width), lambda i: (i, 0))
    lanes = pl.BlockSpec((1, tile), lambda i: (0, i))
    return pl.pallas_call(
        functools.partial(adam_kernel, model_width),
        grid=(owned_rows // tile,),
        in_specs=[lanes] + [rows] * 3 + [lanes] * len(row_sums),
        out_specs=[rows] * 3,
        out_shape=[jax.ShapeDtypeStruct((owned_rows, width), F32)] * 3,
        compiler_params=pltpu.CompilerParams(vmem_limit_bytes=VMEM_BYTES),
        cost_estimate=pl.CostEstimate(flops=row_grad.size, bytes_accessed=0, transcendentals=0),
        name="adam",
    )(row_tier.reshape(1, -1), adam_mean, adam_second, row_grad, *row_sums)


def on_device(
    retrieved,
    branch_states,
    out_grad,
    key_weight,
    value_weight,
    key_grad_acc,
    value_grad_acc,
    row_index,
    row_tier,
    adam_mean,
    adam_second,
):
    tok_count, key_count, width = branch_states.shape
    groups = lax.axis_size("group")
    shards = lax.axis_size("tensor")
    model_width = width * shards
    owned_rows = adam_mean.shape[0]
    half = tok_count // HALVES
    me = lax.axis_index("group")
    line = lax.axis_index("tensor")
    order = ring_order(shards)
    behind = np.zeros((shards, shards), np.int32)
    for spot, device in enumerate(order):
        behind[device] = [order[(spot - step) % shards] for step in range(shards)]
    plan = jnp.concatenate(
        [
            lax.dynamic_index_in_dim(jnp.asarray(behind), line, 0, False),
            jnp.arange(groups, dtype=jnp.int32) ^ me,
        ]
    )

    by_row = lambda x: lax.optimization_barrier(jnp.transpose(x, (1, 0, 2)))
    rows = by_row(retrieved)
    chains = []
    for h in range(HALVES):
        chains.append([sum_rows(h, rows, chains[-1] if chains else ())])
    states, grads, _ = lax.optimization_barrier((branch_states, out_grad, chains[-1][0]))
    states, grads = by_row(states), by_row(grads)
    for step in range(shards - 1):
        if step == min(1, shards - 2):
            slot_index, slot_row = route(
                row_index.T, owned_rows, groups, (chains[-1][0], states, grads)
            )
            incoming_rows = lax.all_to_all(
                slot_row, "group", split_axis=0, concat_axis=0, tiled=True
            ).reshape(1, -1)
            chains[0][-1] = after(chains[0][-1], incoming_rows)
        for chain in chains:
            if step == shards - 2 and chain is chains[-1]:
                weights = join_weights(
                    plan, key_weight, value_weight, (incoming_rows, states, grads)
                )
                chain[-1] = after(chain[-1], weights)
            chain.append(ring_pass(chain[-1], "tensor"))
    acc, turned = forward_early(plan, weights, [chain[:-1] for chain in chains], key_count)
    vals, turned, sums = forward_late(
        plan, weights, [chain[-1] for chain in chains], acc, turned, states, grads
    )
    other_turned = swap_over("group", 1, turned)
    sums = [sums] + others_over("tensor", sums)

    lanes = -(-width // 256) * 128
    cuts = [lanes, width - lanes] if width > lanes else [width]
    joined = cotangents(sums, vals, states, grads, model_width, (other_turned,))
    other_joined = swap_over("group", 1, joined)
    first_term = back(1 % shards, joined, weights, [width])
    passing = [ring_pass(first_term[0], "tensor")]

    shard_rows = model_width // groups
    bits = [1 << k for k in range(1, groups.bit_length() - 1)]
    ways = [bits, bits[::-1]]
    mine, arrived, last, turns = [[], []], {}, (first_term[0],), 0

    def send(way, rel, part):
        bit = next(bit for bit in ways[way] if rel & bit)
        got = swap_over("group", bit, part)
        if rel == bit:
            mine[way].append(got)
        else:
            arrived.setdefault((way, rel ^ bit), []).append(got)

    def in_order(kernel, *args, **more):
        nonlocal last
        result = kernel(*args, after=last, **more)
        last = (result[0] if isinstance(result, (list, tuple)) else result,)
        return result

    def turn(between=()):
        nonlocal turns
        term = in_order(back, (turns + 2) % shards, joined, weights, cuts)
        parts = passing if len(passing) == len(cuts) else passing * len(cuts)
        start = 0
        for k, cut in enumerate(cuts):
            parts[k] = ring_pass(in_order(add_part, parts[k], term[k], start if parts is not passing else 0), "tensor")
            start += cut
            if k < len(between):
                between[k]()
        passing[:] = parts
        turns += 1

    def early_sum(way):
        early = in_order(add, *mine[way][:-1], dtype=F32)
        mine[way] = [early, mine[way][-1]]

    for level in range(len(bits), -1, -1):
        waiting = []
        for rel in range(0, groups, 2):
            if bin(rel).count("1") != level:
                continue
            follows = rel != groups - 2
            product = in_order(
                outer, shards + rel, plan, shard_rows, joined, other_joined, turned, other_turned
            )
            for way in range(2):
                if rel == 0:
                    mine[way].insert(0, product[way])
                elif (way, rel) in arrived:
                    waiting.append((way, rel, product[way]))
                else:
                    send(way, rel, product[way])
            if follows and rel and turns < shards - 3:
                turn()
        for way, rel, part in waiting:
            send(way, rel, in_order(add, part, *arrived.pop((way, rel))))
    own_term = in_order(back, 0, joined, weights, cuts)
    marks = in_order(mark_slots, slot_index, groups * CAP)
    sums_to_do = [functools.partial(early_sum, way) for way in range(2)]
    while turns < shards - 2:
        turn(sums_to_do if True else ())
        sums_to_do = () if True else sums_to_do
    weight_sum = jnp.concatenate([sum(p.astype(F32) for p in parts) for parts in mine], axis=0)
    key_grad = key_grad_acc + jnp.stack(
        [weight_sum[:, j * width : (j + 1) * width] for j in range(key_count)]
    )
    value_grad = value_grad_acc + weight_sum[:, key_count * width :]

    outgoing = pick_rows(marks, passing, own_term)
    incoming = lax.all_to_all(
        outgoing.reshape(groups, CAP, -1), "group", split_axis=0, concat_axis=0, tiled=True
    ).reshape(groups * CAP, -1)
    row_grad, row_part = place_rows(
        incoming_rows, incoming, owned_rows, (key_grad, value_grad)
    )
    row_sums = [row_part] + others_over("tensor", row_part)
    new_mean, new_second, row_step = adam(
        model_width, row_tier, adam_mean, adam_second, row_grad, row_sums
    )
    return (key_grad, value_grad, new_mean, new_second, row_step)


def solution(mesh):
    return jax.shard_map(
        on_device,
        mesh=mesh,
        in_specs=(
            P("group", None, "tensor"),
            P("group", None, "tensor"),
            P("group", None, "tensor"),
            P(None, None, "tensor"),
            P(None, "tensor"),
            P(None, "group", "tensor"),
            P("group", "tensor"),
            P("group", None),
            P("group"),
            P("group", "tensor"),
            P("group", "tensor"),
        ),
        out_specs=(
            P(None, "group", "tensor"),
            P("group", "tensor"),
            P("group", "tensor"),
            P("group", "tensor"),
            P("group", "tensor"),
        ),
        check_vma=False,
    )
```

```python
import functools

import jax
import jax.numpy as jnp
import numpy as np
from jax import lax
from jax.experimental import pallas as pl
from jax.experimental.pallas import tpu as pltpu
from jax.sharding import PartitionSpec as P

CAP = 128
SCALE = 10
HALVES = 2
VMEM_BYTES = 20 * 1024 * 1024


EPS_NORM = 1e-06
EPS_ADAM = 1e-08
FIRST_BIAS = 1.0 - 0.9**10
SECOND_BIAS = 1.0 - 0.95**10

F32, BF16 = jnp.float32, jnp.bfloat16


VMEM = pl.BlockSpec(memory_space=pltpu.VMEM)
SMEM = pl.BlockSpec(memory_space=pltpu.SMEM)
ANY = pl.BlockSpec(memory_space=pl.ANY)
NT = (((1,), (1,)), ((), ()))


def call(kernel, name, in_specs, out_shape, args, macs=0, scratch=(), aliases=None, after=()):
    count = len(args)

    def body(*refs):
        kernel(*refs[:count], *refs[count + len(after) :])

    return pl.pallas_call(
        body,
        in_specs=in_specs + [ANY] * len(after),
        out_specs=[VMEM] * len(out_shape),
        out_shape=out_shape,
        scratch_shapes=scratch,
        input_output_aliases=aliases or {},
        compiler_params=pltpu.CompilerParams(vmem_limit_bytes=VMEM_BYTES),
        cost_estimate=pl.CostEstimate(flops=macs // SCALE, bytes_accessed=0, transcendentals=0),
        name=name,
    )(*args, *after)


def ring_order(size):
    return list(range(0, size, 2)) + list(range(1, size, 2))[::-1]


def ring_pass(part, axis):
    size = lax.axis_size(axis)
    order = ring_order(size)
    return lax.ppermute(part, axis, [(order[i], order[(i + 1) % size]) for i in range(size)])


def others_over(axis, part):
    size = lax.axis_size(axis)
    return [
        lax.ppermute(part, axis, [(i, i ^ step) for i in range(size)])
        for step in range(1, size)
    ]


def swap_over(axis, bit, part):
    size = lax.axis_size(axis)
    return lax.ppermute(part, axis, [(i, i ^ bit) for i in range(size)])


def after_kernel(*refs):
    del refs


def after(x, *others):
    return pl.pallas_call(
        after_kernel,
        in_specs=[ANY] * (1 + len(others)),
        out_specs=ANY,
        out_shape=jax.ShapeDtypeStruct(x.shape, x.dtype),
        input_output_aliases={0: 0},
        compiler_params=pltpu.CompilerParams(vmem_limit_bytes=1024 * 1024),
        name="after",
    )(x, *others)


def weight_block(ref, rows, j, width):
    if len(ref.shape) == 2:
        return ref[rows, j * width : (j + 1) * width]
    return ref[j, rows]


def join_kernel(plan_ref, key_ref, value_ref, out_ref, sems):
    key_count, model_width, width = key_ref.shape
    copies = []
    for step in range(model_width // width):
        source_rows = pl.ds(pl.multiple_of(plan_ref[step] * width, width), width)
        rows = pl.ds(step * width, width)
        for j in range(key_count + 1):
            source = key_ref.at[j, source_rows, :] if j < key_count else value_ref.at[source_rows, :]
            if len(out_ref.shape) == 2:
                target = out_ref.at[rows, pl.ds(j * width, width)]
            else:
                target = out_ref.at[j, rows, :]
            copies.append(pltpu.make_async_copy(source, target, sems.at[step, j]))
            copies[-1].start()
    for copy in copies:
        copy.wait()


def join_weights(plan, key_weight, value_weight, after):
    key_count, model_width, width = key_weight.shape
    flat = width % 128 == 0
    shape = (model_width, (key_count + 1) * width) if flat else (key_count + 1, model_width, width)
    return call(
        join_kernel,
        "join_weights",
        [SMEM] + [ANY] * 2,
        [jax.ShapeDtypeStruct(shape, BF16)],
        [plan, key_weight, value_weight],
        scratch=[pltpu.SemaphoreType.DMA((model_width // width, key_count + 1))],
        after=after,
    )[0]


def partial_products(parts, weight_ref, first, j):
    width = parts[0].shape[1]
    if len(weight_ref.shape) == 2:
        rows = slice(first * width, (first + len(parts)) * width)
        whole = jnp.concatenate(parts, axis=1) if len(parts) > 1 else parts[0]
        weight = weight_block(weight_ref, rows, j, width)
        return jnp.dot(whole, weight, preferred_element_type=F32)
    return sum(
        jnp.dot(
            part,
            weight_block(weight_ref, slice((first + k) * width, (first + k + 1) * width), j, width),
            preferred_element_type=F32,
        )
        for k, part in enumerate(parts)
    )


def early_kernel(steps, plan_ref, weight_ref, *refs):
    *part_refs, acc_ref, turned_ref = refs
    width = acc_ref.shape[2]
    parts = [
        jnp.concatenate([part_refs[h * steps + step][...] for h in range(HALVES)], axis=0)
        for step in range(steps)
    ]
    for j in range(acc_ref.shape[0]):
        acc_ref[j] = partial_products(parts, weight_ref, 0, j)
    for step in range(steps):
        turned_ref[pl.ds(pl.multiple_of(plan_ref[step] * width, width), width), :] = parts[step].T


def forward_early(plan, weights, chains, key_count):
    steps = len(chains[0])
    half, width = chains[0][0].shape
    tok_count = half * HALVES
    return call(
        functools.partial(early_kernel, steps),
        "forward_early",
        [SMEM] + [VMEM] * (1 + HALVES * steps),
        [
            jax.ShapeDtypeStruct((key_count + 1, tok_count, width), F32),
            jax.ShapeDtypeStruct((weights.shape[-2], tok_count), BF16),
        ],
        [plan, weights] + [part for chain in chains for part in chain],
        macs=tok_count * steps * width * width * (key_count + 1),
    )


def late_kernel(step, plan_ref, weight_ref, *refs):
    part_refs, refs = refs[:HALVES], refs[HALVES:]
    acc_ref, _, state_ref, grad_ref, val_ref, turned_ref, sum_ref = refs
    key_count, tok_count, width = state_ref.shape
    part = jnp.concatenate([ref[...] for ref in part_refs], axis=0)
    row_sum = lambda x: jnp.sum(x, axis=1, keepdims=True)
    sums = [None] * (4 * key_count)
    for j in range(key_count + 1):
        val = acc_ref[j] + partial_products([part], weight_ref, step, j)
        if j == key_count:
            for k in range(key_count):
                sums[3 * key_count + k] = row_sum(grad_ref[k].astype(F32) * val)
            continue
        val_ref[j] = val
        state = state_ref[j].astype(F32)
        sums[j] = row_sum(state * state)
        sums[key_count + j] = row_sum(val * val)
        sums[2 * key_count + j] = row_sum(state * val)
    lane = lax.broadcasted_iota(jnp.int32, (tok_count, 128), 1)
    table = jnp.zeros((tok_count, 128), F32)
    for i, s in enumerate(sums):
        table = jnp.where(lane == i, s, table)
    sum_ref[...] = table.T[: 4 * key_count]
    turned_ref[pl.ds(pl.multiple_of(plan_ref[step] * width, width), width), :] = part.T


def forward_late(plan, weights, parts, acc, turned, states, grads):
    key_count, tok_count, width = states.shape
    return call(
        functools.partial(late_kernel, weights.shape[-2] // width - 1),
        "forward_late",
        [SMEM] + [VMEM] * (5 + HALVES),
        [
            jax.ShapeDtypeStruct(acc.shape, F32),
            jax.ShapeDtypeStruct(turned.shape, BF16),
            jax.ShapeDtypeStruct((4 * key_count, tok_count), F32),
        ],
        [plan, weights, *parts, acc, turned, states, grads],
        macs=tok_count * width * width * (key_count + 1),
        aliases={2 + HALVES: 0, 3 + HALVES: 1},
    )


def cot_kernel(sums_count, model_width, *refs):
    sum_refs, refs = refs[:sums_count], refs[sums_count:]
    val_ref, state_ref, grad_ref, joined_ref = refs
    key_count, tok_count, width = state_ref.shape
    half = tok_count // HALVES
    total = sum_refs[0][...]
    for ref in sum_refs[1:]:
        total = total + ref[...]
    root_width = jnp.sqrt(F32(model_width))
    state_sum, key_sum, cross_dot, out_dot = (
        total[i * key_count : (i + 1) * key_count] for i in range(4)
    )
    state_rs = lax.rsqrt(state_sum / model_width + EPS_NORM)
    key_rs = lax.rsqrt(key_sum / model_width + EPS_NORM)
    scores = cross_dot * state_rs * key_rs / root_width
    gate_val = 1.0 / (1.0 + jnp.exp(-scores))
    dscore = out_dot * gate_val * (1.0 - gate_val)
    lead = key_rs * dscore / root_width
    slope = key_rs * scores / root_width
    factors = jnp.concatenate([lead, state_rs, slope, gate_val], axis=0)
    filler = jnp.zeros((128 - 4 * key_count, half), F32)
    for h in range(HALVES):
        rows = slice(h * half, (h + 1) * half)
        table = jnp.concatenate([factors[:, rows], filler], axis=0).T
        column = lambda kind, j: table[:, kind * key_count + j : kind * key_count + j + 1]
        value_cot = None
        for j in range(key_count):
            state = state_ref[j, rows].astype(F32)
            inner = state * column(1, j) - val_ref[j, rows] * column(2, j)
            joined_ref[rows, j * width : (j + 1) * width] = (column(0, j) * inner).astype(BF16)
            gated = column(3, j) * grad_ref[j, rows].astype(F32)
            value_cot = gated if value_cot is None else value_cot + gated
        joined_ref[rows, key_count * width :] = value_cot.astype(BF16)


def cotangents(sums, vals, states, grads, model_width, after):
    key_count, tok_count, width = states.shape
    return call(
        functools.partial(cot_kernel, len(sums), model_width),
        "cotangents",
        [VMEM] * (len(sums) + 3),
        [jax.ShapeDtypeStruct((tok_count, (key_count + 1) * width), BF16)],
        [*sums, vals, states, grads],
        macs=tok_count * width,
        after=after,
    )[0]


def back_kernel(step, joined_ref, weight_ref, *refs):
    width = sum(ref.shape[1] for ref in refs)
    rows = slice(step * width, (step + 1) * width)
    if len(weight_ref.shape) == 2:
        term = lax.dot_general(
            joined_ref[...], weight_ref[rows], NT, preferred_element_type=F32
        )
    else:
        term = sum(
            lax.dot_general(
                joined_ref[:, j * width : (j + 1) * width],
                weight_ref[j, rows],
                NT,
                preferred_element_type=F32,
            )
            for j in range(weight_ref.shape[0])
        )
    start = 0
    for ref in refs:
        ref[...] = term[:, start : start + ref.shape[1]].astype(BF16)
        start += ref.shape[1]


def back(step, joined, weights, cuts, after=()):
    tok_count, columns = joined.shape
    return call(
        functools.partial(back_kernel, step),
        "back",
        [VMEM] * 2,
        [jax.ShapeDtypeStruct((tok_count, cut), BF16) for cut in cuts],
        [joined, weights],
        macs=tok_count * columns * sum(cuts),
        after=after,
    )


def outer_kernel(
    entry, plan_ref, joined_ref, other_joined_ref, turned_ref, other_turned_ref, *refs
):
    rows = sum(ref.shape[0] for ref in refs)
    block = pl.ds(pl.multiple_of(plan_ref[entry] * rows, rows), rows)
    product = jnp.dot(turned_ref[block, :], joined_ref[...], preferred_element_type=F32)
    product = product + jnp.dot(
        other_turned_ref[block, :], other_joined_ref[...], preferred_element_type=F32
    )
    start = 0
    for ref in refs:
        ref[...] = product[start : start + ref.shape[0]].astype(BF16)
        start += ref.shape[0]


def outer(entry, plan, rows, joined, other_joined, turned, other_turned, after=()):
    tok_count, columns = joined.shape
    return call(
        functools.partial(outer_kernel, entry),
        "outer",
        [SMEM] + [VMEM] * 4,
        [jax.ShapeDtypeStruct((r, columns), BF16) for r in (rows // 2, rows - rows // 2)],
        [plan, joined, other_joined, turned, other_turned],
        macs=2 * rows * tok_count * columns,
        after=after,
    )


def route_kernel(owned_rows, row_ref, slot_ref, out_ref):
    grams, tok_count = row_ref.shape
    groups = out_ref.shape[0]
    nt = functools.partial(lax.dot_general, dimension_numbers=NT, preferred_element_type=F32)
    flag = lambda x: x.astype(F32).astype(BF16)
    before = lax.broadcasted_iota(jnp.int32, (tok_count, tok_count), 0)
    before = flag(before <= lax.broadcasted_iota(jnp.int32, (tok_count, tok_count), 1))
    owners = lax.broadcasted_iota(jnp.int32, (groups, tok_count), 0)
    slots = lax.broadcasted_iota(jnp.int32, (groups * CAP, tok_count), 0)
    taken = jnp.zeros((groups, 1), F32)
    held = jnp.zeros((16, groups * CAP), F32)
    for n in range(grams):
        row = row_ref[n : n + 1, :]
        owner = row // owned_rows
        mine = owners == owner
        count = jnp.dot(flag(mine), before, preferred_element_type=F32) + taken
        taken = count[:, tok_count - 1 :]
        place = jnp.sum(jnp.where(mine, count, 0.0), axis=0, keepdims=True).astype(jnp.int32) - 1
        slot = owner * CAP + place
        slot_ref[n : n + 1, :] = slot
        local = row - owner * owned_rows + 1
        digits = jnp.concatenate([local // 128, local % 128], axis=0).astype(F32)
        digits = jnp.concatenate([digits, jnp.zeros((14, tok_count), F32)], axis=0).astype(BF16)
        held = held + nt(digits, flag(slots == slot))
    found = (held[0:1] * 128.0 + held[1:2]).astype(jnp.int32)
    for group in range(groups):
        out_ref[group : group + 1, :] = found[:, group * CAP : (group + 1) * CAP]


def route(rows, owned_rows, groups, after=()):
    return call(
        functools.partial(route_kernel, owned_rows),
        "route",
        [VMEM],
        [
            jax.ShapeDtypeStruct(rows.shape, jnp.int32),
            jax.ShapeDtypeStruct((groups, CAP), jnp.int32),
        ],
        [rows],
        macs=rows.size * rows.shape[1],
        after=after,
    )


def memory_kernel(h, rows_ref, out_ref):
    half = out_ref.shape[0]
    part = slice(h * half, (h + 1) * half)
    total = rows_ref[0, part].astype(F32)
    for n in range(1, rows_ref.shape[0]):
        total = total + rows_ref[n, part].astype(F32)
    out_ref[...] = total.astype(BF16)


def sum_rows(h, rows, after):
    _, tok_count, width = rows.shape
    return call(
        functools.partial(memory_kernel, h),
        "sum_rows",
        [VMEM],
        [jax.ShapeDtypeStruct((tok_count // HALVES, width), BF16)],
        [rows],
        macs=tok_count * width,
        after=after,
    )[0]


def sum_kernel(*refs):
    total = refs[0][...].astype(F32)
    for ref in refs[1:-1]:
        total = total + ref[...].astype(F32)
    refs[-1][...] = total.astype(refs[-1].dtype)


def add(*parts, after=(), dtype=BF16):
    return call(
        sum_kernel,
        "add",
        [VMEM] * len(parts),
        [jax.ShapeDtypeStruct(parts[0].shape, dtype)],
        parts,
        macs=parts[0].size,
        after=after,
    )[0]


def part_kernel(start, whole_ref, part_ref, out_ref):
    whole = whole_ref[:, start : start + part_ref.shape[1]]
    out_ref[...] = (whole.astype(F32) + part_ref[...].astype(F32)).astype(BF16)


def add_part(whole, part, start, after=()):
    return call(
        functools.partial(part_kernel, start),
        "add_part",
        [VMEM] * 2,
        [jax.ShapeDtypeStruct(part.shape, BF16)],
        [whole, part],
        macs=part.size,
        after=after,
    )[0]


def mark_kernel(entry, plan_ref, slot_ref, out_ref):
    slots = lax.broadcasted_iota(jnp.int32, out_ref.shape, 0) ^ (plan_ref[entry] * CAP)
    marks = sum((slots == slot_ref[n : n + 1, :]).astype(F32) for n in range(slot_ref.shape[0]))
    out_ref[...] = marks.astype(BF16)


def mark_slots(entry, plan, slot_index, slot_count, after=()):
    return call(
        functools.partial(mark_kernel, entry),
        "mark_slots",
        [SMEM, VMEM],
        [jax.ShapeDtypeStruct((slot_count, slot_index.shape[1]), BF16)],
        [plan, slot_index],
        macs=slot_count * slot_index.shape[1],
        after=after,
    )[0]


def pick_kernel(count, mark_ref, *refs):
    out_refs = refs[2 * count :]
    start = 0
    for passing_ref, term_ref in zip(refs[:count], refs[count : 2 * count]):
        total = (passing_ref[...].astype(F32) + term_ref[...].astype(F32)).astype(BF16)
        columns = slice(start, start + total.shape[1])
        product = jnp.dot(mark_ref[...], total, preferred_element_type=F32).astype(BF16)
        for rel, ref in enumerate(out_refs):
            ref[:, columns] = product[rel * CAP : (rel + 1) * CAP]
        start += total.shape[1]


def pick_rows(marks, passing, terms, after):
    slot_count, tok_count = marks.shape
    width = sum(part.shape[1] for part in passing)
    return call(
        functools.partial(pick_kernel, len(passing)),
        "pick_rows",
        [VMEM] * (1 + 2 * len(passing)),
        [jax.ShapeDtypeStruct((CAP, width), BF16)] * (slot_count // CAP),
        [marks, *passing, *terms],
        macs=slot_count * tok_count * width,
        after=after,
    )


def place_kernel(entry, plan_ref, row_ref, *refs):
    *incoming, grad_ref, sum_ref = refs
    rows = lax.broadcasted_iota(jnp.int32, (grad_ref.shape[0], CAP), 0) + 1
    places = []
    for rel in range(len(incoming)):
        source = pl.multiple_of(plan_ref[entry + rel] * CAP, CAP)
        places.append((rows == row_ref[:, pl.ds(source, CAP)]).astype(F32).astype(BF16))
    grad = jnp.dot(
        jnp.concatenate(places, axis=1),
        jnp.concatenate([ref[...] for ref in incoming], axis=0),
        preferred_element_type=F32,
    )
    grad_ref[...] = grad
    sums = jnp.sum(grad * grad, axis=1, keepdims=True)
    sum_ref[...] = jnp.broadcast_to(sums, (sums.shape[0], 128)).T[:1]


def place_rows(entry, plan, incoming_rows, incoming, owned_rows, after):
    width = incoming[0].shape[1]
    return call(
        functools.partial(place_kernel, entry),
        "place_rows",
        [SMEM] + [VMEM] * (1 + len(incoming)),
        [
            jax.ShapeDtypeStruct((owned_rows, width), F32),
            jax.ShapeDtypeStruct((1, owned_rows), F32),
        ],
        [plan, incoming_rows, *incoming],
        macs=incoming_rows.size * width * owned_rows,
        after=after,
    )


def hot_kernel(tier_ref, mean_ref, second_ref, grad_ref, new_mean_ref, new_second_ref, step_ref):
    hot = jnp.broadcast_to((tier_ref[...] == 1).astype(F32), (128, tier_ref.shape[1])).T
    is_hot = hot[:, :1] > 0.5
    grad = grad_ref[...]
    mean_hot = 0.9 * mean_ref[...] + 0.1 * grad
    second_hot = 0.95 * second_ref[...] + 0.05 * grad * grad
    step_hot = mean_hot / FIRST_BIAS / (jnp.sqrt(second_hot / SECOND_BIAS) + EPS_ADAM)
    new_mean_ref[...] = jnp.where(is_hot, mean_hot, mean_ref[...])
    new_second_ref[...] = jnp.where(is_hot, second_hot, second_ref[...])
    step_ref[...] = jnp.where(is_hot, step_hot, grad)


def cold_kernel(model_width, tier_ref, step_ref, *refs):
    *sum_refs, out_ref = refs
    row_sum = sum_refs[0][...]
    for ref in sum_refs[1:]:
        row_sum = row_sum + ref[...]
    cold = lax.rsqrt(row_sum / model_width + EPS_NORM)
    scale = jnp.where(tier_ref[...] == 1, 1.0, cold)
    out_ref[...] = step_ref[...] * jnp.broadcast_to(scale, (128, scale.shape[1])).T[:, :1]


def adam(model_width, row_tier, adam_mean, adam_second, row_grad, row_sums):
    owned_rows, width = row_grad.shape
    tile = 128 if owned_rows % 128 == 0 else owned_rows
    rows = pl.BlockSpec((tile, width), lambda i: (i, 0))
    lanes = pl.BlockSpec((1, tile), lambda i: (0, i))
    tier = row_tier.reshape(1, -1)
    shape = jax.ShapeDtypeStruct((owned_rows, width), F32)
    make = functools.partial(
        pl.pallas_call,
        grid=(owned_rows // tile,),
        compiler_params=pltpu.CompilerParams(vmem_limit_bytes=VMEM_BYTES),
        cost_estimate=pl.CostEstimate(flops=row_grad.size, bytes_accessed=0, transcendentals=0),
    )
    new_mean, new_second, step = make(
        hot_kernel,
        in_specs=[lanes] + [rows] * 3,
        out_specs=[rows] * 3,
        out_shape=[shape] * 3,
        name="adam_hot",
    )(tier, adam_mean, adam_second, row_grad)
    row_step = make(
        functools.partial(cold_kernel, model_width),
        in_specs=[lanes, rows] + [lanes] * len(row_sums),
        out_specs=rows,
        out_shape=shape,
        name="adam_cold",
    )(tier, step, *row_sums)
    return new_mean, new_second, row_step


def on_device(
    retrieved,
    branch_states,
    out_grad,
    key_weight,
    value_weight,
    key_grad_acc,
    value_grad_acc,
    row_index,
    row_tier,
    adam_mean,
    adam_second,
):
    tok_count, key_count, width = branch_states.shape
    groups = lax.axis_size("group")
    shards = lax.axis_size("tensor")
    model_width = width * shards
    owned_rows = adam_mean.shape[0]
    half = tok_count // HALVES
    me = lax.axis_index("group")
    line = lax.axis_index("tensor")
    order = ring_order(shards)
    behind = np.zeros((shards, shards), np.int32)
    for spot, device in enumerate(order):
        behind[device] = [order[(spot - step) % shards] for step in range(shards)]
    plan = jnp.concatenate(
        [
            lax.dynamic_index_in_dim(jnp.asarray(behind), line, 0, False),
            jnp.arange(groups, dtype=jnp.int32) ^ me,
        ]
    )

    by_row = lambda x: lax.optimization_barrier(jnp.transpose(x, (1, 0, 2)))
    rows = by_row(retrieved)
    chains = []
    for h in range(HALVES):
        chains.append([sum_rows(h, rows, chains[-1] if chains else ())])
    states, grads, _ = lax.optimization_barrier((branch_states, out_grad, chains[-1][0]))
    states, grads = by_row(states), by_row(grads)
    for step in range(shards - 1):
        if step == min(1, shards - 2):
            slot_index, slot_row = route(
                row_index.T, owned_rows, groups, (chains[-1][0], states, grads)
            )
            incoming_rows = lax.all_to_all(
                slot_row, "group", split_axis=0, concat_axis=0, tiled=True
            ).reshape(1, -1)
            chains[0][-1] = after(chains[0][-1], incoming_rows)
        for chain in chains:
            if step == shards - 2 and chain is chains[-1]:
                weights = join_weights(
                    plan, key_weight, value_weight, (incoming_rows, states, grads)
                )
                chain[-1] = after(chain[-1], weights)
            chain.append(ring_pass(chain[-1], "tensor"))
    acc, turned = forward_early(plan, weights, [chain[:-1] for chain in chains], key_count)
    vals, turned, sums = forward_late(
        plan, weights, [chain[-1] for chain in chains], acc, turned, states, grads
    )
    other_turned = swap_over("group", 1, turned)
    sums = [sums] + others_over("tensor", sums)

    lanes = -(-width // 256) * 128
    cuts = [lanes, width - lanes] if width > lanes else [width]
    joined = cotangents(sums, vals, states, grads, model_width, (other_turned,))
    other_joined = swap_over("group", 1, joined)
    first_term = back(1 % shards, joined, weights, [width])
    passing = [ring_pass(first_term[0], "tensor")]

    shard_rows = model_width // groups
    bits = [1 << k for k in range(1, groups.bit_length() - 1)]
    ways = [bits, bits[::-1]]
    mine, arrived, last, turns = [[], []], {}, (first_term[0],), 0

    def send(way, rel, part):
        bit = next(bit for bit in ways[way] if rel & bit)
        got = swap_over("group", bit, part)
        if rel == bit:
            mine[way].append(got)
        else:
            arrived.setdefault((way, rel ^ bit), []).append(got)

    def in_order(kernel, *args, **more):
        nonlocal last
        result = kernel(*args, after=last, **more)
        last = (result[0] if isinstance(result, (list, tuple)) else result,)
        return result

    def turn(between=()):
        nonlocal turns
        term = in_order(back, (turns + 2) % shards, joined, weights, cuts)
        parts = passing if len(passing) == len(cuts) else passing * len(cuts)
        start = 0
        for k, cut in enumerate(cuts):
            parts[k] = ring_pass(in_order(add_part, parts[k], term[k], start if parts is not passing else 0), "tensor")
            start += cut
            if k < len(between):
                between[k]()
        for rest in between[len(cuts) :]:
            rest()
        passing[:] = parts
        turns += 1

    def early_sum(way):
        early = in_order(add, *mine[way][:-1], dtype=F32)
        mine[way] = [early, mine[way][-1]]

    for level in range(len(bits), -1, -1):
        waiting = []
        for rel in range(0, groups, 2):
            if bin(rel).count("1") != level:
                continue
            product = in_order(
                outer, shards + rel, plan, shard_rows, joined, other_joined, turned, other_turned
            )
            for way in range(2):
                if rel == 0:
                    mine[way].insert(0, product[way])
                elif (way, rel) in arrived:
                    waiting.append((way, rel, product[way]))
                else:
                    send(way, rel, product[way])
        if 0 < level < len(bits) and turns < shards - 3:
            turn()
        for way, rel, part in waiting:
            send(way, rel, in_order(add, part, *arrived.pop((way, rel))))
    def finish(first):
        nonlocal own_term, marks
        if first:
            own_term = in_order(back, 0, joined, weights, cuts)
            early_sum(0)
        else:
            early_sum(1)
            marks = in_order(mark_slots, shards, plan, slot_index, groups * CAP)

    own_term = marks = None
    while turns < shards - 2:
        turn([functools.partial(finish, k == 0) for k in range(2)] if turns == shards - 3 else ())
    weight_sum = jnp.concatenate([sum(p.astype(F32) for p in parts) for parts in mine], axis=0)
    key_grad = key_grad_acc + jnp.stack(
        [weight_sum[:, j * width : (j + 1) * width] for j in range(key_count)]
    )
    value_grad = value_grad_acc + weight_sum[:, key_count * width :]

    outgoing = pick_rows(marks, passing, own_term, ())
    incoming = [outgoing[0]] + [None] * (groups - 1)
    for rel in range(groups - 1, 0, -1):
        incoming[rel] = swap_over("group", rel, outgoing[rel])
    row_grad, row_part = place_rows(
        shards, plan, incoming_rows, incoming, owned_rows, (key_grad, value_grad)
    )
    row_sums = [row_part] + others_over("tensor", row_part)
    new_mean, new_second, row_step = adam(
        model_width, row_tier, adam_mean, adam_second, row_grad, row_sums
    )
    return (key_grad, value_grad, new_mean, new_second, row_step)


def solution(mesh):
    return jax.shard_map(
        on_device,
        mesh=mesh,
        in_specs=(
            P("group", None, "tensor"),
            P("group", None, "tensor"),
            P("group", None, "tensor"),
            P(None, None, "tensor"),
            P(None, "tensor"),
            P(None, "group", "tensor"),
            P("group", "tensor"),
            P("group", None),
            P("group"),
            P("group", "tensor"),
            P("group", "tensor"),
        ),
        out_specs=(
            P(None, "group", "tensor"),
            P("group", "tensor"),
            P("group", "tensor"),
            P("group", "tensor"),
            P("group", "tensor"),
        ),
        check_vma=False,
    )
```

```python
import functools

import jax
import jax.numpy as jnp
import numpy as np
from jax import lax
from jax.experimental import pallas as pl
from jax.experimental.pallas import tpu as pltpu
from jax.sharding import PartitionSpec as P

CAP = 128
SCALE = 10
HALVES = 2
VMEM_BYTES = 20 * 1024 * 1024


EPS_NORM = 1e-06
EPS_ADAM = 1e-08
FIRST_BIAS = 1.0 - 0.9**10
SECOND_BIAS = 1.0 - 0.95**10

F32, BF16 = jnp.float32, jnp.bfloat16


VMEM = pl.BlockSpec(memory_space=pltpu.VMEM)
SMEM = pl.BlockSpec(memory_space=pltpu.SMEM)
ANY = pl.BlockSpec(memory_space=pl.ANY)
NT = (((1,), (1,)), ((), ()))


def call(kernel, name, in_specs, out_shape, args, macs=0, scratch=(), aliases=None, after=()):
    count = len(args)

    def body(*refs):
        kernel(*refs[:count], *refs[count + len(after) :])

    return pl.pallas_call(
        body,
        in_specs=in_specs + [ANY] * len(after),
        out_specs=[VMEM] * len(out_shape),
        out_shape=out_shape,
        scratch_shapes=scratch,
        input_output_aliases=aliases or {},
        compiler_params=pltpu.CompilerParams(vmem_limit_bytes=VMEM_BYTES),
        cost_estimate=pl.CostEstimate(flops=macs // SCALE, bytes_accessed=0, transcendentals=0),
        name=name,
    )(*args, *after)


def ring_order(size):
    return list(range(0, size, 2)) + list(range(1, size, 2))[::-1]


def ring_pass(part, axis):
    size = lax.axis_size(axis)
    order = ring_order(size)
    return lax.ppermute(part, axis, [(order[i], order[(i + 1) % size]) for i in range(size)])


def others_over(axis, part):
    size = lax.axis_size(axis)
    return [
        lax.ppermute(part, axis, [(i, i ^ step) for i in range(size)])
        for step in range(1, size)
    ]


def swap_over(axis, bit, part):
    size = lax.axis_size(axis)
    return lax.ppermute(part, axis, [(i, i ^ bit) for i in range(size)])


def after_kernel(*refs):
    del refs


def after(x, *others):
    return pl.pallas_call(
        after_kernel,
        in_specs=[ANY] * (1 + len(others)),
        out_specs=ANY,
        out_shape=jax.ShapeDtypeStruct(x.shape, x.dtype),
        input_output_aliases={0: 0},
        compiler_params=pltpu.CompilerParams(vmem_limit_bytes=1024 * 1024),
        name="after",
    )(x, *others)


def weight_block(ref, rows, j, width):
    if len(ref.shape) == 2:
        return ref[rows, j * width : (j + 1) * width]
    return ref[j, rows]


def join_kernel(plan_ref, key_ref, value_ref, out_ref, sems):
    key_count, model_width, width = key_ref.shape
    copies = []
    for step in range(model_width // width):
        source_rows = pl.ds(pl.multiple_of(plan_ref[step] * width, width), width)
        rows = pl.ds(step * width, width)
        for j in range(key_count + 1):
            source = key_ref.at[j, source_rows, :] if j < key_count else value_ref.at[source_rows, :]
            if len(out_ref.shape) == 2:
                target = out_ref.at[rows, pl.ds(j * width, width)]
            else:
                target = out_ref.at[j, rows, :]
            copies.append(pltpu.make_async_copy(source, target, sems.at[step, j]))
            copies[-1].start()
    for copy in copies:
        copy.wait()


def join_weights(plan, key_weight, value_weight, after):
    key_count, model_width, width = key_weight.shape
    flat = width % 128 == 0
    shape = (model_width, (key_count + 1) * width) if flat else (key_count + 1, model_width, width)
    return call(
        join_kernel,
        "join_weights",
        [SMEM] + [ANY] * 2,
        [jax.ShapeDtypeStruct(shape, BF16)],
        [plan, key_weight, value_weight],
        scratch=[pltpu.SemaphoreType.DMA((model_width // width, key_count + 1))],
        after=after,
    )[0]


def partial_products(parts, weight_ref, first, j):
    width = parts[0].shape[1]
    if len(weight_ref.shape) == 2:
        rows = slice(first * width, (first + len(parts)) * width)
        whole = jnp.concatenate(parts, axis=1) if len(parts) > 1 else parts[0]
        weight = weight_block(weight_ref, rows, j, width)
        return jnp.dot(whole, weight, preferred_element_type=F32)
    return sum(
        jnp.dot(
            part,
            weight_block(weight_ref, slice((first + k) * width, (first + k + 1) * width), j, width),
            preferred_element_type=F32,
        )
        for k, part in enumerate(parts)
    )


def early_kernel(steps, plan_ref, weight_ref, *refs):
    *part_refs, acc_ref, turned_ref = refs
    width = acc_ref.shape[2]
    parts = [
        jnp.concatenate([part_refs[h * steps + step][...] for h in range(HALVES)], axis=0)
        for step in range(steps)
    ]
    for j in range(acc_ref.shape[0]):
        acc_ref[j] = partial_products(parts, weight_ref, 0, j)
    for step in range(steps):
        turned_ref[pl.ds(pl.multiple_of(plan_ref[step] * width, width), width), :] = parts[step].T


def forward_early(plan, weights, chains, key_count):
    steps = len(chains[0])
    half, width = chains[0][0].shape
    tok_count = half * HALVES
    return call(
        functools.partial(early_kernel, steps),
        "forward_early",
        [SMEM] + [VMEM] * (1 + HALVES * steps),
        [
            jax.ShapeDtypeStruct((key_count + 1, tok_count, width), F32),
            jax.ShapeDtypeStruct((weights.shape[-2], tok_count), BF16),
        ],
        [plan, weights] + [part for chain in chains for part in chain],
        macs=tok_count * steps * width * width * (key_count + 1),
    )


def late_kernel(h, step, plan_ref, weight_ref, part_ref, acc_ref, _, state_ref, grad_ref, *refs):
    val_ref, turned_ref, sum_ref = refs[h > 0 :]
    half, width = part_ref.shape
    key_count = state_ref.shape[0]
    rows = slice(h * half, (h + 1) * half)
    part = part_ref[...]
    row_sum = lambda x: jnp.sum(x, axis=1, keepdims=True)
    sums = [None] * (4 * key_count)
    for j in range(key_count + 1):
        val = acc_ref[j, rows] + partial_products([part], weight_ref, step, j)
        if j == key_count:
            for k in range(key_count):
                sums[3 * key_count + k] = row_sum(grad_ref[k, rows].astype(F32) * val)
            continue
        val_ref[j, rows] = val
        state = state_ref[j, rows].astype(F32)
        sums[j] = row_sum(state * state)
        sums[key_count + j] = row_sum(val * val)
        sums[2 * key_count + j] = row_sum(state * val)
    lane = lax.broadcasted_iota(jnp.int32, (half, 128), 1)
    table = jnp.zeros((half, 128), F32)
    for i, s in enumerate(sums):
        table = jnp.where(lane == i, s, table)
    if h:
        sum_ref[:, : h * half] = refs[0][...]
    sum_ref[:, rows] = table.T[: 4 * key_count]
    place = pl.multiple_of(plan_ref[step] * width, width)
    turned_ref[pl.ds(place, width), rows] = part.T


def forward_late(h, plan, weights, part, acc, turned, states, grads, before):
    key_count, _, width = states.shape
    half = part.shape[0]
    return call(
        functools.partial(late_kernel, h, weights.shape[-2] // width - 1),
        "forward_late",
        [SMEM] + [VMEM] * (6 + len(before)),
        [
            jax.ShapeDtypeStruct(acc.shape, F32),
            jax.ShapeDtypeStruct(turned.shape, BF16),
            jax.ShapeDtypeStruct((4 * key_count, (h + 1) * half), F32),
        ],
        [plan, weights, part, acc, turned, states, grads, *before],
        macs=half * width * width * (key_count + 1),
        aliases={3: 0, 4: 1},
    )


def cot_kernel(sums_count, model_width, *refs):
    sum_refs, refs = refs[:sums_count], refs[sums_count:]
    val_ref, state_ref, grad_ref, joined_ref = refs
    key_count, tok_count, width = state_ref.shape
    half = tok_count // HALVES
    total = sum_refs[0][...]
    for ref in sum_refs[1:]:
        total = total + ref[...]
    root_width = jnp.sqrt(F32(model_width))
    state_sum, key_sum, cross_dot, out_dot = (
        total[i * key_count : (i + 1) * key_count] for i in range(4)
    )
    state_rs = lax.rsqrt(state_sum / model_width + EPS_NORM)
    key_rs = lax.rsqrt(key_sum / model_width + EPS_NORM)
    scores = cross_dot * state_rs * key_rs / root_width
    gate_val = 1.0 / (1.0 + jnp.exp(-scores))
    dscore = out_dot * gate_val * (1.0 - gate_val)
    lead = key_rs * dscore / root_width
    slope = key_rs * scores / root_width
    factors = jnp.concatenate([lead, state_rs, slope, gate_val], axis=0)
    filler = jnp.zeros((128 - 4 * key_count, half), F32)
    for h in range(HALVES):
        rows = slice(h * half, (h + 1) * half)
        table = jnp.concatenate([factors[:, rows], filler], axis=0).T
        column = lambda kind, j: table[:, kind * key_count + j : kind * key_count + j + 1]
        value_cot = None
        for j in range(key_count):
            state = state_ref[j, rows].astype(F32)
            inner = state * column(1, j) - val_ref[j, rows] * column(2, j)
            joined_ref[rows, j * width : (j + 1) * width] = (column(0, j) * inner).astype(BF16)
            gated = column(3, j) * grad_ref[j, rows].astype(F32)
            value_cot = gated if value_cot is None else value_cot + gated
        joined_ref[rows, key_count * width :] = value_cot.astype(BF16)


def cotangents(sums, vals, states, grads, model_width, after):
    key_count, tok_count, width = states.shape
    return call(
        functools.partial(cot_kernel, len(sums), model_width),
        "cotangents",
        [VMEM] * (len(sums) + 3),
        [jax.ShapeDtypeStruct((tok_count, (key_count + 1) * width), BF16)],
        [*sums, vals, states, grads],
        macs=tok_count * width,
        after=after,
    )[0]


def back_kernel(step, joined_ref, weight_ref, *refs):
    width = sum(ref.shape[1] for ref in refs)
    rows = slice(step * width, (step + 1) * width)
    if len(weight_ref.shape) == 2:
        term = lax.dot_general(
            joined_ref[...], weight_ref[rows], NT, preferred_element_type=F32
        )
    else:
        term = sum(
            lax.dot_general(
                joined_ref[:, j * width : (j + 1) * width],
                weight_ref[j, rows],
                NT,
                preferred_element_type=F32,
            )
            for j in range(weight_ref.shape[0])
        )
    start = 0
    for ref in refs:
        ref[...] = term[:, start : start + ref.shape[1]].astype(BF16)
        start += ref.shape[1]


def back(step, joined, weights, cuts, after=()):
    tok_count, columns = joined.shape
    return call(
        functools.partial(back_kernel, step),
        "back",
        [VMEM] * 2,
        [jax.ShapeDtypeStruct((tok_count, cut), BF16) for cut in cuts],
        [joined, weights],
        macs=tok_count * columns * sum(cuts),
        after=after,
    )


def outer_kernel(
    entry, plan_ref, joined_ref, other_joined_ref, turned_ref, other_turned_ref, *refs
):
    rows = sum(ref.shape[0] for ref in refs)
    block = pl.ds(pl.multiple_of(plan_ref[entry] * rows, rows), rows)
    product = jnp.dot(turned_ref[block, :], joined_ref[...], preferred_element_type=F32)
    product = product + jnp.dot(
        other_turned_ref[block, :], other_joined_ref[...], preferred_element_type=F32
    )
    start = 0
    for ref in refs:
        ref[...] = product[start : start + ref.shape[0]].astype(BF16)
        start += ref.shape[0]


def outer(entry, plan, rows, joined, other_joined, turned, other_turned, after=()):
    tok_count, columns = joined.shape
    return call(
        functools.partial(outer_kernel, entry),
        "outer",
        [SMEM] + [VMEM] * 4,
        [jax.ShapeDtypeStruct((r, columns), BF16) for r in (rows // 2, rows - rows // 2)],
        [plan, joined, other_joined, turned, other_turned],
        macs=2 * rows * tok_count * columns,
        after=after,
    )


def route_kernel(owned_rows, row_ref, slot_ref, out_ref):
    grams, tok_count = row_ref.shape
    groups = out_ref.shape[0]
    nt = functools.partial(lax.dot_general, dimension_numbers=NT, preferred_element_type=F32)
    flag = lambda x: x.astype(F32).astype(BF16)
    before = lax.broadcasted_iota(jnp.int32, (tok_count, tok_count), 0)
    before = flag(before <= lax.broadcasted_iota(jnp.int32, (tok_count, tok_count), 1))
    owners = lax.broadcasted_iota(jnp.int32, (groups, tok_count), 0)
    slots = lax.broadcasted_iota(jnp.int32, (groups * CAP, tok_count), 0)
    taken = jnp.zeros((groups, 1), F32)
    held = jnp.zeros((16, groups * CAP), F32)
    for n in range(grams):
        row = row_ref[n : n + 1, :]
        owner = row // owned_rows
        mine = owners == owner
        count = jnp.dot(flag(mine), before, preferred_element_type=F32) + taken
        taken = count[:, tok_count - 1 :]
        place = jnp.sum(jnp.where(mine, count, 0.0), axis=0, keepdims=True).astype(jnp.int32) - 1
        slot = owner * CAP + place
        slot_ref[n : n + 1, :] = slot
        local = row - owner * owned_rows + 1
        digits = jnp.concatenate([local // 128, local % 128], axis=0).astype(F32)
        digits = jnp.concatenate([digits, jnp.zeros((14, tok_count), F32)], axis=0).astype(BF16)
        held = held + nt(digits, flag(slots == slot))
    found = (held[0:1] * 128.0 + held[1:2]).astype(jnp.int32)
    for group in range(groups):
        out_ref[group : group + 1, :] = found[:, group * CAP : (group + 1) * CAP]


def route(rows, owned_rows, groups, after=()):
    return call(
        functools.partial(route_kernel, owned_rows),
        "route",
        [VMEM],
        [
            jax.ShapeDtypeStruct(rows.shape, jnp.int32),
            jax.ShapeDtypeStruct((groups, CAP), jnp.int32),
        ],
        [rows],
        macs=rows.size * rows.shape[1],
        after=after,
    )


def memory_kernel(h, rows_ref, out_ref):
    half = out_ref.shape[0]
    part = slice(h * half, (h + 1) * half)
    total = rows_ref[0, part].astype(F32)
    for n in range(1, rows_ref.shape[0]):
        total = total + rows_ref[n, part].astype(F32)
    out_ref[...] = total.astype(BF16)


def sum_rows(h, rows, after):
    _, tok_count, width = rows.shape
    return call(
        functools.partial(memory_kernel, h),
        "sum_rows",
        [VMEM],
        [jax.ShapeDtypeStruct((tok_count // HALVES, width), BF16)],
        [rows],
        macs=tok_count * width,
        after=after,
    )[0]


def sum_kernel(*refs):
    total = refs[0][...].astype(F32)
    for ref in refs[1:-1]:
        total = total + ref[...].astype(F32)
    refs[-1][...] = total.astype(refs[-1].dtype)


def add(*parts, after=(), dtype=BF16):
    return call(
        sum_kernel,
        "add",
        [VMEM] * len(parts),
        [jax.ShapeDtypeStruct(parts[0].shape, dtype)],
        parts,
        macs=parts[0].size,
        after=after,
    )[0]


def part_kernel(start, whole_ref, part_ref, out_ref):
    whole = whole_ref[:, start : start + part_ref.shape[1]]
    out_ref[...] = (whole.astype(F32) + part_ref[...].astype(F32)).astype(BF16)


def add_part(whole, part, start, after=()):
    return call(
        functools.partial(part_kernel, start),
        "add_part",
        [VMEM] * 2,
        [jax.ShapeDtypeStruct(part.shape, BF16)],
        [whole, part],
        macs=part.size,
        after=after,
    )[0]


def mark_kernel(entry, plan_ref, slot_ref, out_ref):
    slots = lax.broadcasted_iota(jnp.int32, out_ref.shape, 0) ^ (plan_ref[entry] * CAP)
    marks = sum((slots == slot_ref[n : n + 1, :]).astype(F32) for n in range(slot_ref.shape[0]))
    out_ref[...] = marks.astype(BF16)


def mark_slots(entry, plan, slot_index, slot_count, after=()):
    return call(
        functools.partial(mark_kernel, entry),
        "mark_slots",
        [SMEM, VMEM],
        [jax.ShapeDtypeStruct((slot_count, slot_index.shape[1]), BF16)],
        [plan, slot_index],
        macs=slot_count * slot_index.shape[1],
        after=after,
    )[0]


def pick_kernel(count, mark_ref, *refs):
    out_refs = refs[2 * count :]
    start = 0
    for passing_ref, term_ref in zip(refs[:count], refs[count : 2 * count]):
        total = (passing_ref[...].astype(F32) + term_ref[...].astype(F32)).astype(BF16)
        columns = slice(start, start + total.shape[1])
        product = jnp.dot(mark_ref[...], total, preferred_element_type=F32).astype(BF16)
        for rel, ref in enumerate(out_refs):
            ref[:, columns] = product[rel * CAP : (rel + 1) * CAP]
        start += total.shape[1]


def pick_rows(marks, passing, terms, after):
    slot_count, tok_count = marks.shape
    width = sum(part.shape[1] for part in passing)
    return call(
        functools.partial(pick_kernel, len(passing)),
        "pick_rows",
        [VMEM] * (1 + 2 * len(passing)),
        [jax.ShapeDtypeStruct((CAP, width), BF16)] * (slot_count // CAP),
        [marks, *passing, *terms],
        macs=slot_count * tok_count * width,
        after=after,
    )


def place_kernel(entry, plan_ref, row_ref, *refs):
    *incoming, grad_ref, sum_ref = refs
    rows = lax.broadcasted_iota(jnp.int32, (grad_ref.shape[0], CAP), 0) + 1
    places = []
    for rel in range(len(incoming)):
        source = pl.multiple_of(plan_ref[entry + rel] * CAP, CAP)
        places.append((rows == row_ref[:, pl.ds(source, CAP)]).astype(F32).astype(BF16))
    grad = jnp.dot(
        jnp.concatenate(places, axis=1),
        jnp.concatenate([ref[...] for ref in incoming], axis=0),
        preferred_element_type=F32,
    )
    grad_ref[...] = grad
    sums = jnp.sum(grad * grad, axis=1, keepdims=True)
    sum_ref[...] = jnp.broadcast_to(sums, (sums.shape[0], 128)).T[:1]


def place_rows(entry, plan, incoming_rows, incoming, owned_rows, after):
    width = incoming[0].shape[1]
    return call(
        functools.partial(place_kernel, entry),
        "place_rows",
        [SMEM] + [VMEM] * (1 + len(incoming)),
        [
            jax.ShapeDtypeStruct((owned_rows, width), F32),
            jax.ShapeDtypeStruct((1, owned_rows), F32),
        ],
        [plan, incoming_rows, *incoming],
        macs=incoming_rows.size * width * owned_rows,
        after=after,
    )


def hot_kernel(tier_ref, mean_ref, second_ref, grad_ref, new_mean_ref, new_second_ref, step_ref):
    hot = jnp.broadcast_to((tier_ref[...] == 1).astype(F32), (128, tier_ref.shape[1])).T
    is_hot = hot[:, :1] > 0.5
    grad = grad_ref[...]
    mean_hot = 0.9 * mean_ref[...] + 0.1 * grad
    second_hot = 0.95 * second_ref[...] + 0.05 * grad * grad
    step_hot = mean_hot / FIRST_BIAS / (jnp.sqrt(second_hot / SECOND_BIAS) + EPS_ADAM)
    new_mean_ref[...] = jnp.where(is_hot, mean_hot, mean_ref[...])
    new_second_ref[...] = jnp.where(is_hot, second_hot, second_ref[...])
    step_ref[...] = jnp.where(is_hot, step_hot, grad)


def cold_kernel(model_width, tier_ref, step_ref, *refs):
    *sum_refs, out_ref = refs
    row_sum = sum_refs[0][...]
    for ref in sum_refs[1:]:
        row_sum = row_sum + ref[...]
    cold = lax.rsqrt(row_sum / model_width + EPS_NORM)
    scale = jnp.where(tier_ref[...] == 1, 1.0, cold)
    out_ref[...] = step_ref[...] * jnp.broadcast_to(scale, (128, scale.shape[1])).T[:, :1]


def adam(model_width, row_tier, adam_mean, adam_second, row_grad, row_sums):
    owned_rows, width = row_grad.shape
    tile = 128 if owned_rows % 128 == 0 else owned_rows
    rows = pl.BlockSpec((tile, width), lambda i: (i, 0))
    lanes = pl.BlockSpec((1, tile), lambda i: (0, i))
    tier = row_tier.reshape(1, -1)
    shape = jax.ShapeDtypeStruct((owned_rows, width), F32)
    make = functools.partial(
        pl.pallas_call,
        grid=(owned_rows // tile,),
        compiler_params=pltpu.CompilerParams(vmem_limit_bytes=VMEM_BYTES),
        cost_estimate=pl.CostEstimate(flops=row_grad.size, bytes_accessed=0, transcendentals=0),
    )
    new_mean, new_second, step = make(
        hot_kernel,
        in_specs=[lanes] + [rows] * 3,
        out_specs=[rows] * 3,
        out_shape=[shape] * 3,
        name="adam_hot",
    )(tier, adam_mean, adam_second, row_grad)
    row_step = make(
        functools.partial(cold_kernel, model_width),
        in_specs=[lanes, rows] + [lanes] * len(row_sums),
        out_specs=rows,
        out_shape=shape,
        name="adam_cold",
    )(tier, step, *row_sums)
    return new_mean, new_second, row_step


def on_device(
    retrieved,
    branch_states,
    out_grad,
    key_weight,
    value_weight,
    key_grad_acc,
    value_grad_acc,
    row_index,
    row_tier,
    adam_mean,
    adam_second,
):
    tok_count, key_count, width = branch_states.shape
    groups = lax.axis_size("group")
    shards = lax.axis_size("tensor")
    model_width = width * shards
    owned_rows = adam_mean.shape[0]
    half = tok_count // HALVES
    me = lax.axis_index("group")
    line = lax.axis_index("tensor")
    order = ring_order(shards)
    behind = np.zeros((shards, shards), np.int32)
    for spot, device in enumerate(order):
        behind[device] = [order[(spot - step) % shards] for step in range(shards)]
    plan = jnp.concatenate(
        [
            lax.dynamic_index_in_dim(jnp.asarray(behind), line, 0, False),
            jnp.arange(groups, dtype=jnp.int32) ^ me,
        ]
    )

    by_row = lambda x: lax.optimization_barrier(jnp.transpose(x, (1, 0, 2)))
    rows = by_row(retrieved)
    chains = []
    for h in range(HALVES):
        chains.append([sum_rows(h, rows, chains[-1] if chains else ())])
    states, grads, _ = lax.optimization_barrier((branch_states, out_grad, chains[-1][0]))
    states, grads = by_row(states), by_row(grads)
    for step in range(shards - 1):
        if step == min(1, shards - 2):
            slot_index, slot_row = route(
                row_index.T, owned_rows, groups, (chains[-1][0], states, grads)
            )
            incoming_rows = lax.all_to_all(
                slot_row, "group", split_axis=0, concat_axis=0, tiled=True
            ).reshape(1, -1)
            chains[0][-1] = after(chains[0][-1], incoming_rows)
        for chain in chains:
            if step == shards - 2 and chain is chains[-1]:
                weights = join_weights(
                    plan, key_weight, value_weight, (incoming_rows, states, grads)
                )
                chain[-1] = after(chain[-1], weights)
            chain.append(ring_pass(chain[-1], "tensor"))
    acc, turned = forward_early(plan, weights, [chain[:-1] for chain in chains], key_count)
    sums = []
    for h, chain in enumerate(chains):
        acc, turned, here = forward_late(
            h, plan, weights, chain[-1], acc, turned, states, grads, sums
        )
        sums = [here]
    vals, sums = acc, sums[0]
    other_turned = swap_over("group", 1, turned)
    sums = [sums] + others_over("tensor", sums)

    lanes = -(-width // 256) * 128
    cuts = [lanes, width - lanes] if width > lanes else [width]
    joined = cotangents(sums, vals, states, grads, model_width, (other_turned,))
    other_joined = swap_over("group", 1, joined)
    first_term = back(1 % shards, joined, weights, [width])
    passing = [ring_pass(first_term[0], "tensor")]

    shard_rows = model_width // groups
    bits = [1 << k for k in range(1, groups.bit_length() - 1)]
    ways = [bits, bits[::-1]]
    mine, arrived, last, turns = [[], []], {}, (first_term[0],), 0

    def send(way, rel, part):
        bit = next(bit for bit in ways[way] if rel & bit)
        got = swap_over("group", bit, part)
        if rel == bit:
            mine[way].append(got)
        else:
            arrived.setdefault((way, rel ^ bit), []).append(got)

    def in_order(kernel, *args, **more):
        nonlocal last
        result = kernel(*args, after=last, **more)
        last = (result[0] if isinstance(result, (list, tuple)) else result,)
        return result

    def turn(between=()):
        nonlocal turns
        term = in_order(back, (turns + 2) % shards, joined, weights, cuts)
        parts = passing if len(passing) == len(cuts) else passing * len(cuts)
        start = 0
        for k, cut in enumerate(cuts):
            parts[k] = ring_pass(in_order(add_part, parts[k], term[k], start if parts is not passing else 0), "tensor")
            start += cut
            if k < len(between):
                between[k]()
        for rest in between[len(cuts) :]:
            rest()
        passing[:] = parts
        turns += 1

    def early_sum(way):
        early = in_order(add, *mine[way][:-1], dtype=F32)
        mine[way] = [early, mine[way][-1]]

    for level in range(len(bits), -1, -1):
        waiting = []
        for rel in range(0, groups, 2):
            if bin(rel).count("1") != level:
                continue
            product = in_order(
                outer, shards + rel, plan, shard_rows, joined, other_joined, turned, other_turned
            )
            for way in range(2):
                if rel == 0:
                    mine[way].insert(0, product[way])
                elif (way, rel) in arrived:
                    waiting.append((way, rel, product[way]))
                else:
                    send(way, rel, product[way])
        if 0 < level < len(bits) and turns < shards - 3:
            turn()
        for way, rel, part in waiting:
            send(way, rel, in_order(add, part, *arrived.pop((way, rel))))
    def finish(first):
        nonlocal own_term, marks
        if first:
            own_term = in_order(back, 0, joined, weights, cuts)
            early_sum(0)
        else:
            early_sum(1)
            marks = in_order(mark_slots, shards, plan, slot_index, groups * CAP)

    own_term = marks = None
    while turns < shards - 2:
        turn([functools.partial(finish, k == 0) for k in range(2)] if turns == shards - 3 else ())
    weight_sum = jnp.concatenate([sum(p.astype(F32) for p in parts) for parts in mine], axis=0)
    key_grad = key_grad_acc + jnp.stack(
        [weight_sum[:, j * width : (j + 1) * width] for j in range(key_count)]
    )
    value_grad = value_grad_acc + weight_sum[:, key_count * width :]

    outgoing = pick_rows(marks, passing, own_term, ())
    incoming = [outgoing[0]] + [None] * (groups - 1)
    for rel in range(groups - 1, 0, -1):
        incoming[rel] = swap_over("group", rel, outgoing[rel])
    row_grad, row_part = place_rows(
        shards, plan, incoming_rows, incoming, owned_rows, (key_grad, value_grad)
    )
    row_sums = [row_part] + others_over("tensor", row_part)
    new_mean, new_second, row_step = adam(
        model_width, row_tier, adam_mean, adam_second, row_grad, row_sums
    )
    return (key_grad, value_grad, new_mean, new_second, row_step)


def solution(mesh):
    return jax.shard_map(
        on_device,
        mesh=mesh,
        in_specs=(
            P("group", None, "tensor"),
            P("group", None, "tensor"),
            P("group", None, "tensor"),
            P(None, None, "tensor"),
            P(None, "tensor"),
            P(None, "group", "tensor"),
            P("group", "tensor"),
            P("group", None),
            P("group"),
            P("group", "tensor"),
            P("group", "tensor"),
        ),
        out_specs=(
            P(None, "group", "tensor"),
            P("group", "tensor"),
            P("group", "tensor"),
            P("group", "tensor"),
            P("group", "tensor"),
        ),
        check_vma=False,
    )
```

```python
import functools

import jax
import jax.numpy as jnp
import numpy as np
from jax import lax
from jax.experimental import pallas as pl
from jax.experimental.pallas import tpu as pltpu
from jax.sharding import PartitionSpec as P

CAP = 128
SCALE = 10
HALVES = 2
VMEM_BYTES = 20 * 1024 * 1024


EPS_NORM = 1e-06
EPS_ADAM = 1e-08
FIRST_BIAS = 1.0 - 0.9**10
SECOND_BIAS = 1.0 - 0.95**10

F32, BF16 = jnp.float32, jnp.bfloat16


VMEM = pl.BlockSpec(memory_space=pltpu.VMEM)
SMEM = pl.BlockSpec(memory_space=pltpu.SMEM)
ANY = pl.BlockSpec(memory_space=pl.ANY)
NT = (((1,), (1,)), ((), ()))


def call(kernel, name, in_specs, out_shape, args, macs=0, scratch=(), aliases=None, after=()):
    count = len(args)

    def body(*refs):
        kernel(*refs[:count], *refs[count + len(after) :])

    return pl.pallas_call(
        body,
        in_specs=in_specs + [ANY] * len(after),
        out_specs=[VMEM] * len(out_shape),
        out_shape=out_shape,
        scratch_shapes=scratch,
        input_output_aliases=aliases or {},
        compiler_params=pltpu.CompilerParams(vmem_limit_bytes=VMEM_BYTES),
        cost_estimate=pl.CostEstimate(flops=macs // SCALE, bytes_accessed=0, transcendentals=0),
        name=name,
    )(*args, *after)


def ring_order(size):
    return list(range(0, size, 2)) + list(range(1, size, 2))[::-1]


def ring_pass(part, axis):
    size = lax.axis_size(axis)
    order = ring_order(size)
    return lax.ppermute(part, axis, [(order[i], order[(i + 1) % size]) for i in range(size)])


def others_over(axis, part):
    size = lax.axis_size(axis)
    return [
        lax.ppermute(part, axis, [(i, i ^ step) for i in range(size)])
        for step in range(1, size)
    ]


def swap_over(axis, bit, part):
    size = lax.axis_size(axis)
    return lax.ppermute(part, axis, [(i, i ^ bit) for i in range(size)])


def after_kernel(*refs):
    del refs


def after(x, *others):
    return pl.pallas_call(
        after_kernel,
        in_specs=[ANY] * (1 + len(others)),
        out_specs=ANY,
        out_shape=jax.ShapeDtypeStruct(x.shape, x.dtype),
        input_output_aliases={0: 0},
        compiler_params=pltpu.CompilerParams(vmem_limit_bytes=1024 * 1024),
        name="after",
    )(x, *others)


def weight_block(ref, rows, j, width):
    if len(ref.shape) == 2:
        return ref[rows, j * width : (j + 1) * width]
    return ref[j, rows]


def join_kernel(plan_ref, key_ref, value_ref, out_ref, sems):
    key_count, model_width, width = key_ref.shape
    copies = []
    for step in range(model_width // width):
        source_rows = pl.ds(pl.multiple_of(plan_ref[step] * width, width), width)
        rows = pl.ds(step * width, width)
        for j in range(key_count + 1):
            source = key_ref.at[j, source_rows, :] if j < key_count else value_ref.at[source_rows, :]
            if len(out_ref.shape) == 2:
                target = out_ref.at[rows, pl.ds(j * width, width)]
            else:
                target = out_ref.at[j, rows, :]
            copies.append(pltpu.make_async_copy(source, target, sems.at[step, j]))
            copies[-1].start()
    for copy in copies:
        copy.wait()


def join_weights(plan, key_weight, value_weight, after):
    key_count, model_width, width = key_weight.shape
    flat = width % 128 == 0
    shape = (model_width, (key_count + 1) * width) if flat else (key_count + 1, model_width, width)
    return call(
        join_kernel,
        "join_weights",
        [SMEM] + [ANY] * 2,
        [jax.ShapeDtypeStruct(shape, BF16)],
        [plan, key_weight, value_weight],
        scratch=[pltpu.SemaphoreType.DMA((model_width // width, key_count + 1))],
        after=after,
    )[0]


def partial_products(parts, weight_ref, first, j):
    width = parts[0].shape[1]
    if len(weight_ref.shape) == 2:
        rows = slice(first * width, (first + len(parts)) * width)
        whole = jnp.concatenate(parts, axis=1) if len(parts) > 1 else parts[0]
        weight = weight_block(weight_ref, rows, j, width)
        return jnp.dot(whole, weight, preferred_element_type=F32)
    return sum(
        jnp.dot(
            part,
            weight_block(weight_ref, slice((first + k) * width, (first + k + 1) * width), j, width),
            preferred_element_type=F32,
        )
        for k, part in enumerate(parts)
    )


def early_kernel(steps, plan_ref, weight_ref, *refs):
    *part_refs, acc_ref, turned_ref = refs
    width = acc_ref.shape[2]
    parts = [
        jnp.concatenate([part_refs[h * steps + step][...] for h in range(HALVES)], axis=0)
        for step in range(steps)
    ]
    for j in range(acc_ref.shape[0]):
        acc_ref[j] = partial_products(parts, weight_ref, 0, j)
    for step in range(steps):
        turned_ref[pl.ds(pl.multiple_of(plan_ref[step] * width, width), width), :] = parts[step].T


def forward_early(plan, weights, chains, key_count):
    steps = len(chains[0])
    half, width = chains[0][0].shape
    tok_count = half * HALVES
    return call(
        functools.partial(early_kernel, steps),
        "forward_early",
        [SMEM] + [VMEM] * (1 + HALVES * steps),
        [
            jax.ShapeDtypeStruct((key_count + 1, tok_count, width), F32),
            jax.ShapeDtypeStruct((weights.shape[-2], tok_count), BF16),
        ],
        [plan, weights] + [part for chain in chains for part in chain],
        macs=tok_count * steps * width * width * (key_count + 1),
    )


def late_kernel(h, step, plan_ref, weight_ref, part_ref, acc_ref, _, state_ref, grad_ref, *refs):
    val_ref, turned_ref, sum_ref = refs[h > 0 :]
    half, width = part_ref.shape
    key_count = state_ref.shape[0]
    rows = slice(h * half, (h + 1) * half)
    part = part_ref[...]
    row_sum = lambda x: jnp.sum(x, axis=1, keepdims=True)
    sums = [None] * (4 * key_count)
    for j in range(key_count + 1):
        val = acc_ref[j, rows] + partial_products([part], weight_ref, step, j)
        if j == key_count:
            for k in range(key_count):
                sums[3 * key_count + k] = row_sum(grad_ref[k, rows].astype(F32) * val)
            continue
        val_ref[j, rows] = val
        state = state_ref[j, rows].astype(F32)
        sums[j] = row_sum(state * state)
        sums[key_count + j] = row_sum(val * val)
        sums[2 * key_count + j] = row_sum(state * val)
    lane = lax.broadcasted_iota(jnp.int32, (half, 128), 1)
    table = jnp.zeros((half, 128), F32)
    for i, s in enumerate(sums):
        table = jnp.where(lane == i, s, table)
    if h:
        sum_ref[:, : h * half] = refs[0][...]
    sum_ref[:, rows] = table.T[: 4 * key_count]
    place = pl.multiple_of(plan_ref[step] * width, width)
    turned_ref[pl.ds(place, width), rows] = part.T


def forward_late(h, plan, weights, part, acc, turned, states, grads, before):
    key_count, _, width = states.shape
    half = part.shape[0]
    return call(
        functools.partial(late_kernel, h, weights.shape[-2] // width - 1),
        "forward_late",
        [SMEM] + [VMEM] * (6 + len(before)),
        [
            jax.ShapeDtypeStruct(acc.shape, F32),
            jax.ShapeDtypeStruct(turned.shape, BF16),
            jax.ShapeDtypeStruct((4 * key_count, (h + 1) * half), F32),
        ],
        [plan, weights, part, acc, turned, states, grads, *before],
        macs=half * width * width * (key_count + 1),
        aliases={3: 0, 4: 1},
    )


def cot_kernel(sums_count, model_width, *refs):
    sum_refs, refs = refs[:sums_count], refs[sums_count:]
    val_ref, state_ref, grad_ref, joined_ref = refs
    key_count, tok_count, width = state_ref.shape
    half = tok_count // HALVES
    total = sum_refs[0][...]
    for ref in sum_refs[1:]:
        total = total + ref[...]
    root_width = jnp.sqrt(F32(model_width))
    state_sum, key_sum, cross_dot, out_dot = (
        total[i * key_count : (i + 1) * key_count] for i in range(4)
    )
    state_rs = lax.rsqrt(state_sum / model_width + EPS_NORM)
    key_rs = lax.rsqrt(key_sum / model_width + EPS_NORM)
    scores = cross_dot * state_rs * key_rs / root_width
    gate_val = 1.0 / (1.0 + jnp.exp(-scores))
    dscore = out_dot * gate_val * (1.0 - gate_val)
    lead = key_rs * dscore / root_width
    slope = key_rs * scores / root_width
    factors = jnp.concatenate([lead, state_rs, slope, gate_val], axis=0)
    filler = jnp.zeros((128 - 4 * key_count, half), F32)
    for h in range(HALVES):
        rows = slice(h * half, (h + 1) * half)
        table = jnp.concatenate([factors[:, rows], filler], axis=0).T
        column = lambda kind, j: table[:, kind * key_count + j : kind * key_count + j + 1]
        value_cot = None
        for j in range(key_count):
            state = state_ref[j, rows].astype(F32)
            inner = state * column(1, j) - val_ref[j, rows] * column(2, j)
            joined_ref[rows, j * width : (j + 1) * width] = (column(0, j) * inner).astype(BF16)
            gated = column(3, j) * grad_ref[j, rows].astype(F32)
            value_cot = gated if value_cot is None else value_cot + gated
        joined_ref[rows, key_count * width :] = value_cot.astype(BF16)


def cotangents(sums, vals, states, grads, model_width, after):
    key_count, tok_count, width = states.shape
    return call(
        functools.partial(cot_kernel, len(sums), model_width),
        "cotangents",
        [VMEM] * (len(sums) + 3),
        [jax.ShapeDtypeStruct((tok_count, (key_count + 1) * width), BF16)],
        [*sums, vals, states, grads],
        macs=tok_count * width,
        after=after,
    )[0]


def back_kernel(step, joined_ref, weight_ref, *refs):
    width = sum(ref.shape[1] for ref in refs)
    rows = slice(step * width, (step + 1) * width)
    if len(weight_ref.shape) == 2:
        term = lax.dot_general(
            joined_ref[...], weight_ref[rows], NT, preferred_element_type=F32
        )
    else:
        term = sum(
            lax.dot_general(
                joined_ref[:, j * width : (j + 1) * width],
                weight_ref[j, rows],
                NT,
                preferred_element_type=F32,
            )
            for j in range(weight_ref.shape[0])
        )
    start = 0
    for ref in refs:
        ref[...] = term[:, start : start + ref.shape[1]].astype(BF16)
        start += ref.shape[1]


def back(step, joined, weights, cuts, after=()):
    tok_count, columns = joined.shape
    return call(
        functools.partial(back_kernel, step),
        "back",
        [VMEM] * 2,
        [jax.ShapeDtypeStruct((tok_count, cut), BF16) for cut in cuts],
        [joined, weights],
        macs=tok_count * columns * sum(cuts),
        after=after,
    )


def outer_kernel(
    entry, plan_ref, joined_ref, other_joined_ref, turned_ref, other_turned_ref, *refs
):
    rows = sum(ref.shape[0] for ref in refs)
    block = pl.ds(pl.multiple_of(plan_ref[entry] * rows, rows), rows)
    product = jnp.dot(turned_ref[block, :], joined_ref[...], preferred_element_type=F32)
    product = product + jnp.dot(
        other_turned_ref[block, :], other_joined_ref[...], preferred_element_type=F32
    )
    start = 0
    for ref in refs:
        ref[...] = product[start : start + ref.shape[0]].astype(BF16)
        start += ref.shape[0]


def outer(entry, plan, rows, joined, other_joined, turned, other_turned, after=()):
    tok_count, columns = joined.shape
    return call(
        functools.partial(outer_kernel, entry),
        "outer",
        [SMEM] + [VMEM] * 4,
        [jax.ShapeDtypeStruct((r, columns), BF16) for r in (rows // 2, rows - rows // 2)],
        [plan, joined, other_joined, turned, other_turned],
        macs=2 * rows * tok_count * columns,
        after=after,
    )


def route_kernel(owned_rows, row_ref, slot_ref, out_ref):
    grams, tok_count = row_ref.shape
    groups = out_ref.shape[0]
    nt = functools.partial(lax.dot_general, dimension_numbers=NT, preferred_element_type=F32)
    flag = lambda x: x.astype(F32).astype(BF16)
    before = lax.broadcasted_iota(jnp.int32, (tok_count, tok_count), 0)
    before = flag(before <= lax.broadcasted_iota(jnp.int32, (tok_count, tok_count), 1))
    owners = lax.broadcasted_iota(jnp.int32, (groups, tok_count), 0)
    slots = lax.broadcasted_iota(jnp.int32, (groups * CAP, tok_count), 0)
    taken = jnp.zeros((groups, 1), F32)
    held = jnp.zeros((16, groups * CAP), F32)
    for n in range(grams):
        row = row_ref[n : n + 1, :]
        owner = row // owned_rows
        mine = owners == owner
        count = jnp.dot(flag(mine), before, preferred_element_type=F32) + taken
        taken = count[:, tok_count - 1 :]
        place = jnp.sum(jnp.where(mine, count, 0.0), axis=0, keepdims=True).astype(jnp.int32) - 1
        slot = owner * CAP + place
        slot_ref[n : n + 1, :] = slot
        local = row - owner * owned_rows + 1
        digits = jnp.concatenate([local // 128, local % 128], axis=0).astype(F32)
        digits = jnp.concatenate([digits, jnp.zeros((14, tok_count), F32)], axis=0).astype(BF16)
        held = held + nt(digits, flag(slots == slot))
    found = (held[0:1] * 128.0 + held[1:2]).astype(jnp.int32)
    for group in range(groups):
        out_ref[group : group + 1, :] = found[:, group * CAP : (group + 1) * CAP]


def route(rows, owned_rows, groups, after=()):
    return call(
        functools.partial(route_kernel, owned_rows),
        "route",
        [VMEM],
        [
            jax.ShapeDtypeStruct(rows.shape, jnp.int32),
            jax.ShapeDtypeStruct((groups, CAP), jnp.int32),
        ],
        [rows],
        macs=rows.size * rows.shape[1],
        after=after,
    )


def memory_kernel(h, rows_ref, out_ref):
    half = out_ref.shape[0]
    part = slice(h * half, (h + 1) * half)
    total = rows_ref[0, part].astype(F32)
    for n in range(1, rows_ref.shape[0]):
        total = total + rows_ref[n, part].astype(F32)
    out_ref[...] = total.astype(BF16)


def sum_rows(h, rows, after):
    _, tok_count, width = rows.shape
    return call(
        functools.partial(memory_kernel, h),
        "sum_rows",
        [VMEM],
        [jax.ShapeDtypeStruct((tok_count // HALVES, width), BF16)],
        [rows],
        macs=tok_count * width,
        after=after,
    )[0]


def sum_kernel(*refs):
    total = refs[0][...].astype(F32)
    for ref in refs[1:-1]:
        total = total + ref[...].astype(F32)
    refs[-1][...] = total.astype(refs[-1].dtype)


def add(*parts, after=(), dtype=BF16):
    return call(
        sum_kernel,
        "add",
        [VMEM] * len(parts),
        [jax.ShapeDtypeStruct(parts[0].shape, dtype)],
        parts,
        macs=parts[0].size,
        after=after,
    )[0]


def part_kernel(start, whole_ref, part_ref, out_ref):
    whole = whole_ref[:, start : start + part_ref.shape[1]]
    out_ref[...] = (whole.astype(F32) + part_ref[...].astype(F32)).astype(BF16)


def add_part(whole, part, start, after=()):
    return call(
        functools.partial(part_kernel, start),
        "add_part",
        [VMEM] * 2,
        [jax.ShapeDtypeStruct(part.shape, BF16)],
        [whole, part],
        macs=part.size,
        after=after,
    )[0]


def mark_kernel(entry, plan_ref, slot_ref, out_ref):
    slots = lax.broadcasted_iota(jnp.int32, out_ref.shape, 0) ^ (plan_ref[entry] * CAP)
    marks = sum((slots == slot_ref[n : n + 1, :]).astype(F32) for n in range(slot_ref.shape[0]))
    out_ref[...] = marks.astype(BF16)


def mark_slots(entry, plan, slot_index, slot_count, after=()):
    return call(
        functools.partial(mark_kernel, entry),
        "mark_slots",
        [SMEM, VMEM],
        [jax.ShapeDtypeStruct((slot_count, slot_index.shape[1]), BF16)],
        [plan, slot_index],
        macs=slot_count * slot_index.shape[1],
        after=after,
    )[0]


def pick_kernel(count, mark_ref, *refs):
    out_refs = refs[2 * count :]
    start = 0
    for passing_ref, term_ref in zip(refs[:count], refs[count : 2 * count]):
        total = (passing_ref[...].astype(F32) + term_ref[...].astype(F32)).astype(BF16)
        columns = slice(start, start + total.shape[1])
        product = jnp.dot(mark_ref[...], total, preferred_element_type=F32).astype(BF16)
        for rel, ref in enumerate(out_refs):
            ref[:, columns] = product[rel * CAP : (rel + 1) * CAP]
        start += total.shape[1]


def pick_rows(marks, passing, terms, after):
    slot_count, tok_count = marks.shape
    width = sum(part.shape[1] for part in passing)
    return call(
        functools.partial(pick_kernel, len(passing)),
        "pick_rows",
        [VMEM] * (1 + 2 * len(passing)),
        [jax.ShapeDtypeStruct((CAP, width), BF16)] * (slot_count // CAP),
        [marks, *passing, *terms],
        macs=slot_count * tok_count * width,
        after=after,
    )


def place_kernel(entry, plan_ref, row_ref, *refs):
    *incoming, grad_ref, sum_ref = refs
    rows = lax.broadcasted_iota(jnp.int32, (grad_ref.shape[0], CAP), 0) + 1
    places = []
    for rel in range(len(incoming)):
        source = pl.multiple_of(plan_ref[entry + rel] * CAP, CAP)
        places.append((rows == row_ref[:, pl.ds(source, CAP)]).astype(F32).astype(BF16))
    grad = jnp.dot(
        jnp.concatenate(places, axis=1),
        jnp.concatenate([ref[...] for ref in incoming], axis=0),
        preferred_element_type=F32,
    )
    grad_ref[...] = grad
    sums = jnp.sum(grad * grad, axis=1, keepdims=True)
    sum_ref[...] = jnp.broadcast_to(sums, (sums.shape[0], 128)).T[:1]


def place_rows(entry, plan, incoming_rows, incoming, owned_rows, after):
    width = incoming[0].shape[1]
    return call(
        functools.partial(place_kernel, entry),
        "place_rows",
        [SMEM] + [VMEM] * (1 + len(incoming)),
        [
            jax.ShapeDtypeStruct((owned_rows, width), F32),
            jax.ShapeDtypeStruct((1, owned_rows), F32),
        ],
        [plan, incoming_rows, *incoming],
        macs=incoming_rows.size * width * owned_rows,
        after=after,
    )


def hot_kernel(tier_ref, mean_ref, second_ref, grad_ref, new_mean_ref, new_second_ref, step_ref):
    hot = jnp.broadcast_to((tier_ref[...] == 1).astype(F32), (128, tier_ref.shape[1])).T
    is_hot = hot[:, :1] > 0.5
    grad = grad_ref[...]
    mean_hot = 0.9 * mean_ref[...] + 0.1 * grad
    second_hot = 0.95 * second_ref[...] + 0.05 * grad * grad
    step_hot = mean_hot / FIRST_BIAS / (jnp.sqrt(second_hot / SECOND_BIAS) + EPS_ADAM)
    new_mean_ref[...] = jnp.where(is_hot, mean_hot, mean_ref[...])
    new_second_ref[...] = jnp.where(is_hot, second_hot, second_ref[...])
    step_ref[...] = jnp.where(is_hot, step_hot, grad)


def cold_kernel(model_width, tier_ref, step_ref, *refs):
    *sum_refs, out_ref = refs
    row_sum = sum_refs[0][...]
    for ref in sum_refs[1:]:
        row_sum = row_sum + ref[...]
    cold = lax.rsqrt(row_sum / model_width + EPS_NORM)
    scale = jnp.where(tier_ref[...] == 1, 1.0, cold)
    out_ref[...] = step_ref[...] * jnp.broadcast_to(scale, (128, scale.shape[1])).T[:, :1]


def adam(model_width, row_tier, adam_mean, adam_second, row_grad, row_sums):
    owned_rows, width = row_grad.shape
    tile = 128 if owned_rows % 128 == 0 else owned_rows
    rows = pl.BlockSpec((tile, width), lambda i: (i, 0))
    lanes = pl.BlockSpec((1, tile), lambda i: (0, i))
    tier = row_tier.reshape(1, -1)
    shape = jax.ShapeDtypeStruct((owned_rows, width), F32)
    make = functools.partial(
        pl.pallas_call,
        grid=(owned_rows // tile,),
        compiler_params=pltpu.CompilerParams(vmem_limit_bytes=VMEM_BYTES),
        cost_estimate=pl.CostEstimate(flops=row_grad.size, bytes_accessed=0, transcendentals=0),
    )
    new_mean, new_second, step = make(
        hot_kernel,
        in_specs=[lanes] + [rows] * 3,
        out_specs=[rows] * 3,
        out_shape=[shape] * 3,
        name="adam_hot",
    )(tier, adam_mean, adam_second, row_grad)
    row_step = make(
        functools.partial(cold_kernel, model_width),
        in_specs=[lanes, rows] + [lanes] * len(row_sums),
        out_specs=rows,
        out_shape=shape,
        name="adam_cold",
    )(tier, step, *row_sums)
    return new_mean, new_second, row_step


def on_device(
    retrieved,
    branch_states,
    out_grad,
    key_weight,
    value_weight,
    key_grad_acc,
    value_grad_acc,
    row_index,
    row_tier,
    adam_mean,
    adam_second,
):
    tok_count, key_count, width = branch_states.shape
    groups = lax.axis_size("group")
    shards = lax.axis_size("tensor")
    model_width = width * shards
    owned_rows = adam_mean.shape[0]
    half = tok_count // HALVES
    me = lax.axis_index("group")
    line = lax.axis_index("tensor")
    order = ring_order(shards)
    behind = np.zeros((shards, shards), np.int32)
    for spot, device in enumerate(order):
        behind[device] = [order[(spot - step) % shards] for step in range(shards)]
    plan = jnp.concatenate(
        [
            lax.dynamic_index_in_dim(jnp.asarray(behind), line, 0, False),
            jnp.arange(groups, dtype=jnp.int32) ^ me,
        ]
    )

    by_row = lambda x: lax.optimization_barrier(jnp.transpose(x, (1, 0, 2)))
    rows = by_row(retrieved)
    chains = []
    for h in range(HALVES):
        chains.append([sum_rows(h, rows, chains[-1] if chains else ())])
    states, grads, _ = lax.optimization_barrier((branch_states, out_grad, chains[-1][0]))
    states, grads = by_row(states), by_row(grads)
    for step in range(shards - 1):
        if step == min(1, shards - 2):
            slot_index, slot_row = route(
                row_index.T, owned_rows, groups, (chains[-1][0], states, grads)
            )
            incoming_rows = lax.all_to_all(
                slot_row, "group", split_axis=0, concat_axis=0, tiled=True
            ).reshape(1, -1)
            chains[0][-1] = after(chains[0][-1], incoming_rows)
        for chain in chains:
            if step == shards - 2 and chain is chains[-1]:
                weights = join_weights(
                    plan, key_weight, value_weight, (incoming_rows, states, grads)
                )
                chain[-1] = after(chain[-1], weights)
            chain.append(ring_pass(chain[-1], "tensor"))
    acc, turned = forward_early(plan, weights, [chain[:-1] for chain in chains], key_count)
    sums = []
    for h, chain in enumerate(chains):
        acc, turned, here = forward_late(
            h, plan, weights, chain[-1], acc, turned, states, grads, sums
        )
        sums = [here]
    vals, sums = acc, sums[0]
    other_turned = swap_over("group", 1, turned)
    sums = [sums] + others_over("tensor", sums)

    lanes = -(-width // 256) * 128
    cuts = [lanes, width - lanes] if width > lanes else [width]
    joined = cotangents(sums, vals, states, grads, model_width, (other_turned,))
    other_joined = swap_over("group", 1, joined)
    first_term = back(1 % shards, joined, weights, [width])
    passing = [ring_pass(first_term[0], "tensor")]

    shard_rows = model_width // groups
    bits = [1 << k for k in range(1, groups.bit_length() - 1)]
    ways = [bits, bits[::-1]]
    mine, arrived, last, turns = [[], []], {}, (first_term[0],), 0

    def send(way, rel, part):
        bit = next(bit for bit in ways[way] if rel & bit)
        got = swap_over("group", bit, part)
        if rel == bit:
            mine[way].append(got)
        else:
            arrived.setdefault((way, rel ^ bit), []).append(got)

    def in_order(kernel, *args, **more):
        nonlocal last
        result = kernel(*args, after=last, **more)
        last = (result[0] if isinstance(result, (list, tuple)) else result,)
        return result

    def turn(between=()):
        nonlocal turns
        term = in_order(back, (turns + 2) % shards, joined, weights, cuts)
        parts = passing if len(passing) == len(cuts) else passing * len(cuts)
        start = 0
        for k, cut in enumerate(cuts):
            parts[k] = ring_pass(in_order(add_part, parts[k], term[k], start if parts is not passing else 0), "tensor")
            start += cut
            if k < len(between):
                between[k]()
        for rest in between[len(cuts) :]:
            rest()
        passing[:] = parts
        turns += 1

    def early_sum(way):
        early = in_order(add, *mine[way][:-1], dtype=F32)
        mine[way] = [early, mine[way][-1]]

    for level in range(len(bits), -1, -1):
        waiting = []
        for rel in range(0, groups, 2):
            if bin(rel).count("1") != level:
                continue
            product = in_order(
                outer, shards + rel, plan, shard_rows, joined, other_joined, turned, other_turned
            )
            for way in range(2):
                if rel == 0:
                    mine[way].insert(0, product[way])
                elif (way, rel) in arrived:
                    waiting.append((way, rel, product[way]))
                else:
                    send(way, rel, product[way])
        if 0 < level < len(bits) and turns < shards - 3:
            turn()
        for way, rel, part in waiting:
            send(way, rel, in_order(add, part, *arrived.pop((way, rel))))
    def finish(first):
        nonlocal own_term, marks
        if first:
            own_term = in_order(back, 0, joined, weights, cuts)
            early_sum(0)
        else:
            early_sum(1)
            marks = in_order(mark_slots, shards, plan, slot_index, groups * CAP)

    own_term = marks = None
    while turns < shards - 2:
        turn()
    finish(True)
    finish(False)
    weight_sum = jnp.concatenate([sum(p.astype(F32) for p in parts) for parts in mine], axis=0)
    key_grad = key_grad_acc + jnp.stack(
        [weight_sum[:, j * width : (j + 1) * width] for j in range(key_count)]
    )
    value_grad = value_grad_acc + weight_sum[:, key_count * width :]

    outgoing = pick_rows(marks, passing, own_term, ())
    incoming = [outgoing[0]] + [None] * (groups - 1)
    for rel in range(1, groups):
        incoming[rel] = swap_over("group", rel, outgoing[rel])
    row_grad, row_part = place_rows(
        shards, plan, incoming_rows, incoming, owned_rows, (key_grad, value_grad)
    )
    row_sums = [row_part] + others_over("tensor", row_part)
    new_mean, new_second, row_step = adam(
        model_width, row_tier, adam_mean, adam_second, row_grad, row_sums
    )
    return (key_grad, value_grad, new_mean, new_second, row_step)


def solution(mesh):
    return jax.shard_map(
        on_device,
        mesh=mesh,
        in_specs=(
            P("group", None, "tensor"),
            P("group", None, "tensor"),
            P("group", None, "tensor"),
            P(None, None, "tensor"),
            P(None, "tensor"),
            P(None, "group", "tensor"),
            P("group", "tensor"),
            P("group", None),
            P("group"),
            P("group", "tensor"),
            P("group", "tensor"),
        ),
        out_specs=(
            P(None, "group", "tensor"),
            P("group", "tensor"),
            P("group", "tensor"),
            P("group", "tensor"),
            P("group", "tensor"),
        ),
        check_vma=False,
    )
```
